32 devices in a mesh: dp: 8 (over y, x, core), mp: 4 (over z).
Axes of the slice: x: 2, y: 2, z: 4, core: 2. Of those that a mesh axis runs over, the one named last changes fastest.
Arguments:
- tokens: bfloat16 [8192, 1024], P(('dp', 'mp')), may hold values from -6 to 6
- seg_ids: int32 [8192], P('dp'), may hold values from 0 to 4, as said below
- cotangent: bfloat16 [8192, 1024], P(('dp', 'mp')), may hold values from -6 to 6
- first_gain: float32 [1024], replicated, may hold values from 0.1 to 1.9
- first_shift: float32 [1024], replicated, may hold values from -3 to 3
- project_weight: bfloat16 [3, 1024, 1024], P(None, None, 'mp'), may hold values from -0.1875 to 0.1875
- project_bias: float32 [3, 1024], P(None, 'mp'), may hold values from -3 to 3
- out_weight: bfloat16 [1024, 1024], P('mp'), may hold values from -0.5 to 0.5
- out_bias: float32 [1024], replicated, may hold values from -3 to 3
- second_gain: float32 [1024], replicated, may hold values from 0.1 to 1.9
- second_shift: float32 [1024], replicated, may hold values from -3 to 3
- up_weight: bfloat16 [1024, 4096], P(None, 'mp'), may hold values from -0.1875 to 0.1875
- up_bias: float32 [4096], P('mp'), may hold values from -3 to 3
- down_weight: bfloat16 [4096, 1024], P('mp'), may hold values from -0.125 to 0.125
- down_bias: float32 [1024], replicated, may hold values from -3 to 3
Outputs:
- output: bfloat16 [8192, 1024], P(('dp', 'mp'))
- tokens_grad: bfloat16 [8192, 1024], P(('dp', 'mp'))
- first_gain_grad: float32 [1024], replicated
- first_shift_grad: float32 [1024], replicated
- project_weight_grad: float32 [3, 1024, 1024], P(None, None, 'mp')
- project_bias_grad: float32 [3, 1024], P(None, 'mp')
- out_weight_grad: float32 [1024, 1024], P('mp')
- out_bias_grad: float32 [1024], replicated
- second_gain_grad: float32 [1024], replicated
- second_shift_grad: float32 [1024], replicated
- up_weight_grad: float32 [1024, 4096], P(None, 'mp')
- up_bias_grad: float32 [4096], P('mp')
- down_weight_grad: float32 [4096, 1024], P('mp')
- down_bias_grad: float32 [1024], replicated
The draws below stay inside these ranges and needn't reach their ends.
Inputs may be any that keep to these rules, and one draw needn't show every extreme that they name: `seg_ids`: within a segment the numbers never fall; equal numbers mark one document, and in every segment one document runs from the segment's first quarter through its third quarter.
All inputs are finite; a program needn't handle non-finite values.
Results may differ from the reference program's by a relative error of at most 0.018.
Values may be sent and summed in bfloat16 or wider, within the bound.
A program may use at most 128 MiB of HBM per device.

```python
import math
import jax
import jax.numpy as jnp
from jax import lax

D = 1024
HEADS = 8
HD = 128
FF = 4096
ROWS = 256
SEG = 1024
TOKENS = 8192


def draw_seg_ids(key, part):
    key = jax.random.fold_in(key, 11)
    count = TOKENS // SEG
    keys = jax.random.split(key, 4)
    first = jax.random.randint(keys[0], (count, 1), 2, ROWS)
    leading = jax.random.randint(keys[1], (count, 1), 1, first)
    late = jax.random.randint(keys[2], (count, 1), 3 * ROWS, SEG)
    final = jax.random.randint(keys[3], (count, 1), late, SEG)
    places = jnp.arange(SEG, dtype=jnp.int32)[None, :]
    numbers = (places >= leading).astype(jnp.int32) + (places >= first).astype(jnp.int32)
    numbers = numbers + (places >= late).astype(jnp.int32) + (places >= final).astype(jnp.int32)
    return numbers.reshape(TOKENS).astype(jnp.int32)


def block_scale(rng, dims, cuts, smallest, high):
    def one(position, shards_of):
        heights = jax.random.uniform(jax.random.fold_in(jax.random.fold_in(rng, 6), position), (shards_of,), jnp.float32, smallest / len(cuts), high / len(cuts))
        return jnp.repeat(jnp.exp(heights), dims[position] // shards_of).reshape((-1,) + (1,) * (len(dims) - position - 1))

    level = one(*cuts[0])
    for cut in cuts[1:]:
        level = level * one(*cut)
    return level


def noise(stream_key, dims, width, reach, cuts=(), kind=jnp.bfloat16):
    array = jax.random.normal(stream_key, dims, jnp.float32) * width
    if len(cuts) > 0:
        array = block_scale(stream_key, dims, cuts, -0.22, 0.18) * array
    return jnp.clip(array, min=-reach, max=reach).astype(kind)


def setup_inputs(seed: int = 0) -> dict:
    streams_of = jax.random.split(jax.random.key(seed), 16)
    return {
        "tokens": noise(streams_of[0], (TOKENS, D), 1.0, 6.0, ((0, 32),)),
        "seg_ids": draw_seg_ids(jax.random.fold_in(streams_of[15], 71), 0),
        "cotangent": noise(streams_of[2], (TOKENS, D), 1.0, 6.0, ((0, 32),)),
        "first_gain": jnp.clip(1.0 + 0.18 * jax.random.normal(streams_of[3], (D,), jnp.float32), 0.1, 1.9),
        "first_shift": noise(streams_of[4], (D,), 0.5, 3.0, (), jnp.float32),
        "project_weight": noise(streams_of[5], (3, D, D), D ** -0.5, 0.1875, ((2, 4),)),
        "project_bias": noise(streams_of[6], (3, D), 0.5, 3.0, ((1, 4),), jnp.float32),
        "out_weight": noise(streams_of[7], (D, D), (D // 8) ** -0.5, 0.5, ((0, 4),)),
        "out_bias": noise(streams_of[8], (D,), 0.5, 3.0, (), jnp.float32),
        "second_gain": jnp.clip(1.0 + 0.18 * jax.random.normal(streams_of[9], (D,), jnp.float32), 0.1, 1.9),
        "second_shift": noise(streams_of[10], (D,), 0.5, 3.0, (), jnp.float32),
        "up_weight": noise(streams_of[11], (D, FF), D ** -0.5, 0.1875, ((1, 4),)),
        "up_bias": noise(streams_of[12], (FF,), 0.5, 3.0, ((0, 4),), jnp.float32),
        "down_weight": noise(streams_of[13], (FF, D), (FF // 2) ** -0.5, 0.125, ((0, 4),)),
        "down_bias": noise(streams_of[14], (D,), 0.5, 3.0, (), jnp.float32),
    }


EPS = 1e-05
HIGH = lax.Precision.HIGHEST

@jax.custom_vjp
def low(v):
    return lax.optimization_barrier(v.astype(jnp.bfloat16)).astype(jnp.float32)

@jax.custom_vjp
def low_back(v):
    return v

def low_keep(v):
    return (low(v), None)

def low_pass(kept, grad):
    return (grad,)

def back_keep(v):
    return (v, None)

def back_low(kept, grad):
    return (low(grad),)
low.defvjp(low_keep, low_pass)
low_back.defvjp(back_keep, back_low)

def layer_norm(values, gain, shift):
    mean = lax.optimization_barrier(jnp.mean(values, -1, keepdims=True))
    centered = values - mean
    var = lax.optimization_barrier(jnp.mean(centered * centered, -1, keepdims=True))
    return centered * lax.rsqrt(var + EPS) * gain + shift

def smooth(values):
    return jax.nn.gelu(values, approximate=True)

def layer(inputs, doc_ids, first_gain, first_shift, project_weight, project_bias, out_weight, out_bias, second_gain, second_shift, up_weight, up_bias, down_weight, down_bias):
    length = inputs.shape[0]
    first = low(layer_norm(inputs, first_gain, first_shift))
    mixed = jnp.einsum('sd,tdc->tsc', first, project_weight, precision=HIGH) + project_bias[:, None, :]
    mixed = low_back(low(mixed))
    queries = mixed[0].reshape(length, HEADS, HD)
    keys_all = mixed[1].reshape(length, HEADS, HD)
    values_all = mixed[2].reshape(length, HEADS, HD)
    factor = 1.0 / math.sqrt(HD)
    span = min(512, length)
    places = jnp.arange(length, dtype=jnp.int32)
    starts = (jnp.arange(length // span, dtype=jnp.int32) * span).astype(jnp.int32)

    def one_block(start):
        query_block = lax.dynamic_slice_in_dim(queries, start, span, 0)
        doc_query = lax.dynamic_slice_in_dim(doc_ids, start, span, 0)
        place_query = start + jnp.arange(span, dtype=jnp.int32)
        scores = jnp.einsum('qhd,khd->hqk', query_block, keys_all, precision=HIGH) * factor
        scores = low_back(scores)
        allowed = (doc_query[:, None] == doc_ids[None, :]) & (place_query[:, None] >= places[None, :])
        scores = jnp.where(allowed[None], scores, -1e+30)
        peak = lax.optimization_barrier(jnp.max(scores, -1, keepdims=True))
        expo = jnp.exp(scores - peak)
        probs = expo / lax.optimization_barrier(jnp.sum(expo, -1, keepdims=True))
        return jnp.einsum('hqk,khd->qhd', low(probs), values_all, precision=HIGH)
    context = lax.map(jax.checkpoint(one_block), starts).reshape(length, HEADS * HD)
    context = low_back(low(context))
    middle = inputs + low_back(jnp.dot(context, out_weight, precision=HIGH) + out_bias)
    second = low(layer_norm(middle, second_gain, second_shift))
    pre = low_back(jnp.dot(second, up_weight, precision=HIGH) + up_bias)
    hidden = low(smooth(pre))
    return middle + low_back(jnp.dot(hidden, down_weight, precision=HIGH) + down_bias)

def reference(tokens, seg_ids, cotangent, first_gain, first_shift, project_weight, project_bias, out_weight, out_bias, second_gain, second_shift, up_weight, up_bias, down_weight, down_bias):
    params = (first_gain, first_shift, project_weight, project_bias, out_weight, out_bias, second_gain, second_shift, up_weight, up_bias, down_weight, down_bias)
    params = tuple((p.astype(jnp.float32) for p in params))
    count = tokens.shape[0] // SEG
    inputs = tokens.astype(jnp.float32).reshape(count, SEG, D)
    grads_in = cotangent.astype(jnp.float32).reshape(count, SEG, D)
    doc_all = seg_ids.reshape(count, SEG)

    def step(totals, item):
        segment, doc_ids, seg_grad = item

        def local(values, *weights):
            return layer(values, doc_ids, *weights)
        result, pull = jax.vjp(local, segment, *params)
        grads = pull(seg_grad)
        totals = tuple((a + b for a, b in zip(totals, grads[1:])))
        return (totals, (result, grads[0]))
    zeros = tuple((jnp.zeros_like(p) for p in params))
    totals, (results, input_grads) = lax.scan(step, zeros, (inputs, doc_all, grads_in))
    output = results.reshape(-1, D).astype(jnp.bfloat16)
    tokens_grad = input_grads.reshape(-1, D).astype(jnp.bfloat16)
    return (output, tokens_grad, totals[0], totals[1], totals[2], totals[3], totals[4], totals[5], totals[6], totals[7], totals[8], totals[9], totals[10], totals[11])
```

```python
import math

import jax
import jax.numpy as jnp
from jax import lax
from jax.experimental import pallas as pl
from jax.experimental.pallas import tpu as pltpu
from jax.sharding import PartitionSpec as P

HD = 128
EPS = 1e-05
BF = jnp.bfloat16
F32 = jnp.float32
MESH = pl.DeviceIdType.MESH
VMEM = pltpu.VMEM
DMA = pltpu.SemaphoreType.DMA


def mm(left, right):
    return jnp.dot(left, right, preferred_element_type=F32)


def mm_nt(left, right):
    return lax.dot_general(left, right, (((1,), (1,)), ((), ())), preferred_element_type=F32)


def mm_tn(left, right):
    return lax.dot_general(left, right, (((0,), (0,)), ((), ())), preferred_element_type=F32)


class Place:
    def __init__(self):
        self.z = lax.axis_index("mp")
        self.dp = lax.axis_index("dp")
        self.d = lax.rem(self.dp, 8)
        self.base = self.dp - self.d
        self.core = lax.rem(self.d, 2)
        self.bit_x = lax.rem(self.d // 2, 2)
        self.bit_y = self.d // 4
        self.sibling = self.d + 1 - 2 * self.core
        step_x = 2 - 4 * self.bit_x
        step_y = 4 - 8 * self.bit_y
        self.chips = (self.d + step_x, self.d + step_y, self.d + step_x + step_y)

    def along(self, z):
        return {"dp": self.dp, "mp": z}

    def plane(self, d):
        return {"dp": self.base + d, "mp": self.z}


def remote(src, dst, ss, rs, device):
    return pltpu.make_async_remote_copy(
        src_ref=src, dst_ref=dst, send_sem=ss, recv_sem=rs, device_id=device, device_id_type=MESH
    )


def barrier(devices):
    sem = pltpu.get_barrier_semaphore()
    for device in devices:
        pl.semaphore_signal(sem, 1, device_id=device, device_id_type=MESH)
    return lambda: pl.semaphore_wait(sem, len(devices))


def norm(values):
    mean = jnp.mean(values, -1, keepdims=True)
    centered = values - mean
    var = jnp.mean(centered * centered, -1, keepdims=True)
    scale = lax.rsqrt(var + EPS)
    return centered * scale, scale


class Line:
    def __init__(self, place, buf, ss, rs, pieces):
        self.p, self.buf, self.ss, self.rs, self.pieces = place, buf, ss, rs, pieces
        self.rows = buf.shape[1] // pieces

    def _copy(self, s, c, target, slot):
        view = self.buf.at[s, pl.ds(c * self.rows, self.rows)]
        return remote(view, view, self.ss.at[slot, c], self.rs.at[s, c], self.p.along(target))

    def _each(self, c, act):
        z = self.p.z
        for slot, off in enumerate((1, -1, 2, -2)):
            if off > 0:
                ok = z < 4 - off
            else:
                ok = z >= -off

            @pl.when(ok)
            def _():
                act(self._copy(z, c, z + off, slot))

    def send(self, c):
        self._each(c, lambda copy: copy.start())

    def _passed(self, c, act):
        z = self.p.z

        @pl.when(z == 2)
        def _():
            act(self._copy(0, c, 3, 4))

        @pl.when(z == 1)
        def _():
            act(self._copy(3, c, 0, 4))

    def order(self, k):
        return lax.rem(self.p.z + k * (1 - 2 * (self.p.z // 2)) + 4, 4)

    def take(self, k):
        s = self.order(k)
        for c in range(self.pieces):
            self._copy(s, c, self.p.z, 0).wait_recv()
            if k == 2:
                self._passed(c, lambda copy: copy.start())
        return s

    def finish(self):
        for c in range(self.pieces):
            self._each(c, lambda copy: copy.wait_send())
            self._passed(c, lambda copy: copy.wait_send())


def softmax_block(mixed, h, r, share, rows, segc, segr, factor):
    width = (r + 1) * rows
    top = r * rows
    q = mixed[top : top + rows, h * HD : (h + 1) * HD]
    k = mixed[0:width, share + h * HD : share + (h + 1) * HD]
    scores = mm_nt(q, k) * factor
    place_q = top + lax.broadcasted_iota(jnp.int32, (rows, width), 0)
    place_k = lax.broadcasted_iota(jnp.int32, (rows, width), 1)
    allowed = (segc[top : top + rows, :] == segr[:, 0:width]) & (place_q >= place_k)
    return jnp.where(allowed, scores, -1e30)


def front(
    x_ref, segr, segc, g1, b1, wq, bq, ow, ob, g2, b2,
    first_out, mixed_out, own_out, ctx_out, lse_out, middle_out, second_out,
    first, mixed, own, ctx, outw, lse,
    ss_first, rs_first, ss_ctx, rs_ctx, ss_wz, rs_wz, ss_wp, rs_wp, ss_ws, rs_ws, sem_out,
):
    p = Place()
    z = p.z
    rows, width = x_ref.shape
    share = wq.shape[2]
    heads = share // HD
    factor = 1.0 / math.sqrt(HD)
    slab = ow.shape[0] // 8
    others = [lax.rem(z + k, 4) for k in (1, 2, 3)]
    enter = barrier([p.along(t) for t in others] + [p.plane(t) for t in p.chips] + [p.plane(p.sibling)])
    line = Line(p, first, ss_first, rs_first, 2)
    half = rows // 2

    def first_norm(c):
        block = x_ref[c * half : (c + 1) * half, :].astype(F32)
        normed, _ = norm(block)
        first[pl.ds(z, 1), c * half : (c + 1) * half, :] = (normed * g1[...] + b1[...]).astype(BF)[None]

    first_norm(0)
    enter()
    line.send(0)
    first_norm(1)
    line.send(1)

    def slab_z(k, zz):
        return remote(
            ow.at[pl.ds(p.d * slab, slab)], outw.at[z, pl.ds(p.d * slab, slab)],
            ss_wz.at[k], rs_wz.at[z], p.along(zz),
        )

    for k, t in enumerate(others):
        slab_z(k, t).start()
    outw[pl.ds(z, 1)] = ow[...][None]

    def project(s):
        for t in range(3):
            part = mm(first[pl.ds(s, 1)][0], wq[t]) + bq[t : t + 1, :]
            mixed[pl.ds(pl.multiple_of(s * rows, rows), rows), t * share : (t + 1) * share] = part.astype(BF)

    project(z)
    for k in (1, 2):
        project(line.take(k))

    def slab_view(t, who):
        return outw.at[t, pl.ds(who * slab, slab)]

    for k, t in enumerate(others):
        remote(slab_view(t, p.d), slab_view(t, p.d), ss_wz.at[k], rs_wz.at[t], p.along(z)).wait_recv()

    def slab_p(i, k, t):
        return remote(
            slab_view(t, p.d), slab_view(t, p.d), ss_wp.at[i, k], rs_wp.at[i, k], p.plane(p.chips[i])
        )

    for i in range(3):
        for k, t in enumerate(others):
            slab_p(i, k, t).start()
    project(line.take(3))

    def ctx_send(r, k):
        return remote(own.at[r], ctx.at[z], ss_ctx.at[r], rs_ctx.at[z], p.along(r))

    for r in reversed(range(4)):
        for h in range(heads):
            scores = softmax_block(mixed, h, r, share, rows, segc, segr, factor)
            peak = jnp.max(scores, -1, keepdims=True)
            expo = jnp.exp(scores - peak)
            total = jnp.sum(expo, -1, keepdims=True)
            probs = (expo / total).astype(BF)
            v = mixed[0 : (r + 1) * rows, 2 * share + h * HD : 2 * share + (h + 1) * HD]
            own[r, :, h * HD : (h + 1) * HD] = mm(probs, v).astype(BF)
            lse[h, r * rows : (r + 1) * rows, :] = jnp.broadcast_to(peak + jnp.log(total), (rows, HD))

        @pl.when(z != r)
        def _():
            ctx_send(r, 0).start()

        @pl.when(z == r)
        def _():
            ctx[r] = own[r]

        if r == 3:
            def slab_s(i, k, who, t):
                return remote(
                    slab_view(t, who), slab_view(t, who), ss_ws.at[i, k], rs_ws.at[i, k], p.plane(p.sibling)
                )

            for k, t in enumerate(others):
                slab_s(3, k, p.d, t).start()
            for i in range(3):
                for k, t in enumerate(others):
                    remote(
                        slab_view(t, p.chips[i]), slab_view(t, p.chips[i]), ss_wp.at[i, k], rs_wp.at[i, k],
                        p.plane(p.d),
                    ).wait_recv()
                    slab_s(i, k, p.chips[i], t).start()

    for i in range(4):
        who = p.sibling if i == 3 else p.chips[i] + p.sibling - p.d
        for k, t in enumerate(others):
            remote(slab_view(t, who), slab_view(t, who), ss_ws.at[i, k], rs_ws.at[i, k], p.plane(p.d)).wait_recv()

    attended = mm(ctx[pl.ds(z, 1)][0], outw[pl.ds(z, 1)][0])
    for t in others:
        remote(own.at[0], ctx.at[t], ss_ctx.at[0], rs_ctx.at[t], p.along(z)).wait_recv()
        attended = attended + mm(ctx[pl.ds(t, 1)][0], outw[pl.ds(t, 1)][0])
    middle = x_ref[...].astype(F32) + (attended + ob[...])
    middle_out[...] = middle
    normed, _ = norm(middle)
    second_out[...] = (normed * g2[...] + b2[...]).astype(BF)

    outs = [
        pltpu.make_async_copy(a, b, sem_out.at[i])
        for i, (a, b) in enumerate(
            ((first, first_out), (mixed, mixed_out), (own, own_out), (ctx, ctx_out), (lse, lse_out))
        )
    ]
    for copy in outs:
        copy.start()
    line.finish()
    for k, t in enumerate(others):
        slab_z(k, t).wait_send()
        for i in range(3):
            slab_p(i, k, t).wait_send()
            slab_s(i, k, p.chips[i], t).wait_send()
        slab_s(3, k, p.d, t).wait_send()
    for r in range(4):

        @pl.when(z != r)
        def _():
            ctx_send(r, 0).wait_send()

    for copy in outs:
        copy.wait()


def run_front(x, seg_ids, g1, b1, wq, bq, ow, ob, g2, b2):
    rows, width = x.shape
    share = wq.shape[2]
    length = 4 * rows
    vm = pl.BlockSpec(memory_space=VMEM)
    hbm = pl.BlockSpec(memory_space=pl.ANY)
    heads = share // HD
    shapes = [
        ((4, rows, width), BF), ((length, 3 * share), BF), ((4, rows, share), BF), ((4, rows, share), BF),
        ((heads, length, HD), F32), ((rows, width), F32), ((rows, width), BF),
    ]
    return pl.pallas_call(
        front,
        out_shape=[jax.ShapeDtypeStruct(s, t) for s, t in shapes],
        in_specs=[vm] * 11,
        out_specs=[hbm] * 5 + [vm] * 2,
        scratch_shapes=[
            VMEM((4, rows, width), BF), VMEM((length, 3 * share), BF), VMEM((4, rows, share), BF),
            VMEM((4, rows, share), BF), VMEM((4, share, width), BF), VMEM((heads, length, HD), F32),
            DMA((5, 2)), DMA((4, 2)), DMA((4,)), DMA((4,)), DMA((3,)), DMA((4,)),
            DMA((3, 3)), DMA((3, 3)), DMA((4, 3)), DMA((4, 3)), DMA((5,)),
        ],
        compiler_params=pltpu.CompilerParams(collective_id=0, has_side_effects=True, vmem_limit_bytes=60 << 20),
        name="front",
    )(
        x, seg_ids.reshape(1, length), seg_ids.reshape(length, 1), g1.reshape(1, width), b1.reshape(1, width),
        wq, bq, ow, ob.reshape(1, width), g2.reshape(1, width), b2.reshape(1, width),
    )


def layer_norm(values, gain, shift):
    mean = jnp.mean(values, -1, keepdims=True)
    centered = values - mean
    var = jnp.mean(centered * centered, -1, keepdims=True)
    scale = lax.rsqrt(var + EPS)
    normed = centered * scale
    return (normed * gain + shift, normed, scale)


def norm_back(grad, normed, scale, gain):
    gain_grad = jnp.sum(grad * normed, 0)
    shift_grad = jnp.sum(grad, 0)
    scaled = grad * gain
    values_grad = scale * (
        scaled
        - jnp.mean(scaled, -1, keepdims=True)
        - normed * jnp.mean(scaled * normed, -1, keepdims=True)
    )
    return (values_grad, gain_grad, shift_grad)


def smooth(values):
    return jax.nn.gelu(values, approximate=True)


def contract_rows(left, right):
    return lax.dot_general(
        left, right, (((0,), (0,)), ((), ())), preferred_element_type=jnp.float32
    )


def times_transposed(left, right):
    return lax.dot_general(
        left, right, (((1,), (1,)), ((), ())), preferred_element_type=jnp.float32
    )


def masked_scores(query_block, keys_all, doc_query, doc_keys, place_query, place_keys, factor):
    scores = (
        jnp.einsum("qhd,khd->hqk", query_block, keys_all, preferred_element_type=jnp.float32)
        * factor
    )
    allowed = (doc_query[:, None] == doc_keys[None, :]) & (
        place_query[:, None] >= place_keys[None, :]
    )
    return jnp.where(allowed[None], scores, -1e30)


def shards(
    tokens,
    seg_ids,
    cotangent,
    first_gain,
    first_shift,
    project_weight,
    project_bias,
    out_weight,
    out_bias,
    second_gain,
    second_shift,
    up_weight,
    up_bias,
    down_weight,
    down_bias,
):
    rows = tokens.shape[0]
    width = tokens.shape[1]
    length = rows * lax.axis_size("mp")
    share = project_weight.shape[2]
    heads = share // HD
    factor = 1.0 / math.sqrt(HD)
    span = min(512, length)
    count_blocks = length // span
    joined_weight = jnp.transpose(project_weight, (1, 0, 2)).reshape(width, 3 * share)
    joined_bias = project_bias.reshape(3 * share)
    places = jnp.arange(length, dtype=jnp.int32)
    starts = jnp.arange(count_blocks, dtype=jnp.int32) * span
    inputs = tokens.astype(jnp.float32)
    _, first_normed, first_scale = layer_norm(inputs, first_gain, first_shift)
    first_all, mixed, context, ctx_rows, lse, middle, second_low = run_front(
        tokens, seg_ids, first_gain, first_shift, project_weight, project_bias, out_weight, out_bias,
        second_gain, second_shift,
    )
    first_all = first_all.reshape(length, width)
    context = context.reshape(length, share)
    queries = mixed[:, :share].reshape(length, heads, HD)
    keys_all = mixed[:, share : 2 * share].reshape(length, heads, HD)
    values_all = mixed[:, 2 * share :].reshape(length, heads, HD)
    logsum = lse[:, :, 0].reshape(heads, count_blocks, span).transpose(1, 0, 2)
    _, second_normed, second_scale = layer_norm(middle, second_gain, second_shift)
    second_all = lax.all_gather(second_low, "mp", axis=0, tiled=True)
    pre = jnp.dot(second_all, up_weight, preferred_element_type=jnp.float32) + up_bias
    activated, smooth_back = jax.vjp(smooth, pre)
    hidden_low = activated.astype(jnp.bfloat16)
    reduced = lax.psum_scatter(
        jnp.dot(hidden_low, down_weight, preferred_element_type=jnp.float32).astype(jnp.bfloat16),
        "mp",
        scatter_dimension=0,
        tiled=True,
    ).astype(jnp.float32)
    output = (middle + (reduced + down_bias)).astype(jnp.bfloat16)
    grad_output = cotangent.astype(jnp.float32)
    grad_all = lax.all_gather(cotangent, "mp", axis=0, tiled=True)
    down_grad = contract_rows(hidden_low, grad_all)
    hidden_grad = times_transposed(grad_all, down_weight)
    pre_low = smooth_back(hidden_grad)[0].astype(jnp.bfloat16)
    up_grad = contract_rows(second_all, pre_low)
    upbias_grad = jnp.sum(pre_low.astype(jnp.float32), 0)
    up_grad, upbias_grad, down_grad = lax.psum((up_grad, upbias_grad, down_grad), "dp")
    second_grad = lax.psum_scatter(
        times_transposed(pre_low, up_weight).astype(jnp.bfloat16),
        "mp",
        scatter_dimension=0,
        tiled=True,
    ).astype(jnp.float32)
    middle_part, second_gain_grad, second_shift_grad = norm_back(
        second_grad, second_normed, second_scale, second_gain
    )
    middle_grad = grad_output + middle_part
    middle_low = middle_grad.astype(jnp.bfloat16)
    outbias_grad = jnp.sum(middle_low.astype(jnp.float32), 0)
    downbias_grad = jnp.sum(grad_output, 0)
    middle_all = lax.all_gather(middle_low, "mp", axis=0, tiled=True)
    outw_grad = contract_rows(context, middle_all)
    context_grad = (
        times_transposed(middle_all, out_weight).astype(jnp.bfloat16).reshape(length, heads, HD)
    )

    def back_block(carry, item):
        keys_grad, values_grad = carry
        start, block_sum = item
        query_block = lax.dynamic_slice_in_dim(queries, start, span, 0)
        doc_query = lax.dynamic_slice_in_dim(seg_ids, start, span, 0)
        place_query = start + jnp.arange(span, dtype=jnp.int32)
        scores = masked_scores(
            query_block, keys_all, doc_query, seg_ids, place_query, places, factor
        )
        probs = jnp.exp(scores - block_sum[..., None])
        upstream = lax.dynamic_slice_in_dim(context_grad, start, span, 0)
        values_grad = values_grad + jnp.einsum(
            "hqk,qhd->khd", probs.astype(jnp.bfloat16), upstream, preferred_element_type=jnp.float32
        )
        probs_grad = jnp.einsum(
            "qhd,khd->hqk", upstream, values_all, preferred_element_type=jnp.float32
        )
        scores_grad = probs * (probs_grad - jnp.sum(probs * probs_grad, -1, keepdims=True))
        scores_low = scores_grad.astype(jnp.bfloat16)
        query_grad = (
            jnp.einsum("hqk,khd->qhd", scores_low, keys_all, preferred_element_type=jnp.float32)
            * factor
        )
        keys_grad = (
            keys_grad
            + jnp.einsum(
                "hqk,qhd->khd", scores_low, query_block, preferred_element_type=jnp.float32
            )
            * factor
        )
        return ((keys_grad, values_grad), query_grad)

    empty = jnp.zeros((length, heads, HD), jnp.float32)
    (keys_grad, values_grad), query_grad = lax.scan(back_block, (empty, empty), (starts, logsum))
    mixed_low = jnp.concatenate(
        [
            query_grad.reshape(length, share),
            keys_grad.reshape(length, share),
            values_grad.reshape(length, share),
        ],
        1,
    ).astype(jnp.bfloat16)
    project_grad = jnp.transpose(
        contract_rows(first_all, mixed_low).reshape(width, 3, share), (1, 0, 2)
    )
    pbias_grad = jnp.sum(mixed_low.astype(jnp.float32), 0).reshape(3, share)
    first_grad = lax.psum_scatter(
        times_transposed(mixed_low, joined_weight).astype(jnp.bfloat16),
        "mp",
        scatter_dimension=0,
        tiled=True,
    ).astype(jnp.float32)
    input_part, first_gain_grad, first_shift_grad = norm_back(
        first_grad, first_normed, first_scale, first_gain
    )
    tokens_grad = (middle_grad + input_part).astype(jnp.bfloat16)
    project_grad, pbias_grad, outw_grad = lax.psum((project_grad, pbias_grad, outw_grad), "dp")
    (
        first_gain_grad,
        first_shift_grad,
        outbias_grad,
        second_gain_grad,
        second_shift_grad,
        downbias_grad,
    ) = lax.psum(
        (
            first_gain_grad,
            first_shift_grad,
            outbias_grad,
            second_gain_grad,
            second_shift_grad,
            downbias_grad,
        ),
        ("dp", "mp"),
    )
    return (
        output,
        tokens_grad,
        first_gain_grad,
        first_shift_grad,
        project_grad,
        pbias_grad,
        outw_grad,
        outbias_grad,
        second_gain_grad,
        second_shift_grad,
        up_grad,
        upbias_grad,
        down_grad,
        downbias_grad,
    )


def solution(mesh):
    in_specs = (
        P(("dp", "mp"), None),
        P("dp"),
        P(("dp", "mp"), None),
        P(),
        P(),
        P(None, None, "mp"),
        P(None, "mp"),
        P("mp", None),
        P(),
        P(),
        P(),
        P(None, "mp"),
        P("mp"),
        P("mp", None),
        P(),
    )
    out_specs = (
        P(("dp", "mp"), None),
        P(("dp", "mp"), None),
        P(),
        P(),
        P(None, None, "mp"),
        P(None, "mp"),
        P("mp", None),
        P(),
        P(),
        P(),
        P(None, "mp"),
        P("mp"),
        P("mp", None),
        P(),
    )
    return jax.shard_map(shards, mesh=mesh, in_specs=in_specs, out_specs=out_specs, check_vma=False)
```

```python
import math

import jax
import jax.numpy as jnp
from jax import lax
from jax.experimental import pallas as pl
from jax.experimental.pallas import tpu as pltpu
from jax.sharding import PartitionSpec as P

HD = 128
EPS = 1e-05
BF = jnp.bfloat16
F32 = jnp.float32
MESH = pl.DeviceIdType.MESH
VMEM = pltpu.VMEM
DMA = pltpu.SemaphoreType.DMA


def mm(left, right):
    return jnp.dot(left, right, preferred_element_type=F32)


def mm_nt(left, right):
    return lax.dot_general(left, right, (((1,), (1,)), ((), ())), preferred_element_type=F32)


def mm_tn(left, right):
    return lax.dot_general(left, right, (((0,), (0,)), ((), ())), preferred_element_type=F32)


class Place:
    def __init__(self):
        self.z = lax.axis_index("mp")
        self.dp = lax.axis_index("dp")
        self.d = lax.rem(self.dp, 8)
        self.base = self.dp - self.d
        self.core = lax.rem(self.d, 2)
        self.bit_x = lax.rem(self.d // 2, 2)
        self.bit_y = self.d // 4
        self.sibling = self.d + 1 - 2 * self.core
        self.step_x = 2 - 4 * self.bit_x
        self.step_y = 4 - 8 * self.bit_y

    def chip(self, i):
        return self.d + (i % 2) * self.step_x + (i // 2) * self.step_y

    def along(self, z):
        return {"dp": self.dp, "mp": z}

    def plane(self, d):
        return {"dp": self.base + d, "mp": self.z}


def remote(src, dst, ss, rs, device):
    return pltpu.make_async_remote_copy(
        src_ref=src, dst_ref=dst, send_sem=ss, recv_sem=rs, device_id=device, device_id_type=MESH
    )


def barrier(devices):
    sem = pltpu.get_barrier_semaphore()
    for device in devices:
        pl.semaphore_signal(sem, 1, device_id=device, device_id_type=MESH)
    return lambda: pl.semaphore_wait(sem, len(devices))


def norm(values):
    mean = jnp.mean(values, -1, keepdims=True)
    centered = values - mean
    var = jnp.mean(centered * centered, -1, keepdims=True)
    scale = lax.rsqrt(var + EPS)
    return centered * scale, scale


class Line:
    def __init__(self, place, view, source, ss, rs, pieces):
        self.p, self.view, self.source, self.ss, self.rs, self.pieces = place, view, source, ss, rs, pieces

    def _copy(self, s, c, target, slot, source=None):
        view = self.view(s, c)
        source = view if source is None else source
        return remote(source, view, self.ss.at[slot, c], self.rs.at[s, c], self.p.along(target))

    def _each(self, c, act):
        z = self.p.z
        for slot, off in enumerate((1, -1, 2, -2)):
            ok = z < 4 - off if off > 0 else z >= -off

            @pl.when(ok)
            def _():
                act(self._copy(z, c, z + off, slot, self.source(c)))

    def send(self, c):
        self._each(c, lambda copy: copy.start())

    def _passed(self, c, act):
        z = self.p.z

        @pl.when(z == 2)
        def _():
            act(self._copy(0, c, 3, 4))

        @pl.when(z == 1)
        def _():
            act(self._copy(3, c, 0, 4))

    def order(self, k):
        return lax.rem(self.p.z + k * (1 - 2 * (self.p.z // 2)) + 4, 4)

    def take(self, k):
        s = self.order(k)
        for c in range(self.pieces):
            self._copy(s, c, self.p.z, 0).wait_recv()
            if k == 2:
                self._passed(c, lambda copy: copy.start())
        return s

    def finish(self):
        for c in range(self.pieces):
            self._each(c, lambda copy: copy.wait_send())
            self._passed(c, lambda copy: copy.wait_send())


class Plane:
    def __init__(self, place, view, ss, rs):
        self.p, self.view, self.ss, self.rs = place, view, ss, rs

    def _own(self, i):
        p = self.p
        to = p.sibling if i == 0 else p.chip(i)
        return remote(self.view(p.d), self.view(p.d), self.ss.at[i], self.rs.at[i], p.plane(to))

    def _second(self, i, who):
        p = self.p
        return remote(self.view(who), self.view(who), self.ss.at[3 + i], self.rs.at[3 + i], p.plane(p.sibling))

    def send(self):
        for i in (1, 2, 3, 0):
            self._own(i).start()

    def take(self, i):
        p = self.p
        who = p.sibling if i == 0 else p.chip(i)
        remote(self.view(who), self.view(who), self.ss.at[i], self.rs.at[i], p.plane(p.d)).wait_recv()
        if i:
            self._second(i, who).start()

    def take_second(self, i):
        p = self.p
        who = p.chip(i) + p.sibling - p.d
        self._second(i, who).wait_recv()

    def finish(self):
        for i in range(4):
            self._own(i).wait_send()
            if i:
                self._second(i, self.p.chip(i)).wait_send()


def softmax_block(mixed, h, r, share, rows, segc, segr, factor):
    width = (r + 1) * rows
    top = r * rows
    q = mixed[top : top + rows, h * HD : (h + 1) * HD]
    k = mixed[0:width, share + h * HD : share + (h + 1) * HD]
    scores = mm_nt(q, k) * factor
    place_q = top + lax.broadcasted_iota(jnp.int32, (rows, width), 0)
    place_k = lax.broadcasted_iota(jnp.int32, (rows, width), 1)
    allowed = (segc[top : top + rows, :] == segr[:, 0:width]) & (place_q >= place_k)
    return jnp.where(allowed, scores, -1e30)


GELU_A = 0.7978845608
GELU_B = 0.044715


def gelu_parts(v):
    square = v * v
    t = jnp.tanh(GELU_A * v * (1.0 + GELU_B * square))
    half = 0.5 * (1.0 + t)
    slope = half + 0.5 * v * (1.0 - t * t) * (GELU_A * (1.0 + 3.0 * GELU_B * square))
    return v * half, slope


def front(
    x_ref, cot, segr, segc, g1, b1, wq, bq, ow, ob, g2, b2, upw, upb, dww, dwb,
    first_out, mixed_out, own_out, lse_out, dctx_out, ug_out, owg_out, output, dmid_out, dg_out, ubg_out, small_out,
    first, mixed, own, ctx, outw, lse, up, down, ub, dy, second, hidden, dpre,
    ds_part, ds_got, ds_sum, ds_in, o_part, o_got, o_sum, o_in, dg, dg_in, ug, owg, dcs, dctx,
    ss_first, rs_first, ss_ctx, rs_ctx, ss_wz, rs_wz, ss_wp, rs_wp, ss_cot, rs_cot, ss_up, rs_up, ss_dn, rs_dn,
    ss_ub, rs_ub, ss_sec, rs_sec, ss_dg, rs_dg, ss_ds, rs_ds, ss_do, rs_do, ss_og, rs_og, ss_oo, rs_oo,
    ss_dc, rs_dc, sem_out, sem_in,
):
    p = Place()
    z = p.z
    rows, width = x_ref.shape
    share = wq.shape[2]
    heads = share // HD
    factor = 1.0 / math.sqrt(HD)
    slab = ow.shape[0] // 8
    part = upw.shape[1] // 8
    others = [lax.rem(z + k, 4) for k in (1, 2, 3)]
    enter = barrier([p.along(t) for t in others] + [p.plane(p.chip(i)) for i in (1, 2, 3)] + [p.plane(p.sibling)])
    half = rows // 2
    line = Line(
        p, lambda s, c: first.at[s, pl.ds(c * half, half)], lambda c: first.at[z, pl.ds(c * half, half)],
        ss_first, rs_first, 2,
    )

    def first_norm(c):
        block = x_ref[c * half : (c + 1) * half, :].astype(F32)
        normed, _ = norm(block)
        first[pl.ds(z, 1), c * half : (c + 1) * half, :] = (normed * g1[...] + b1[...]).astype(BF)[None]

    first_norm(0)
    enter()
    line.send(0)
    first_norm(1)
    line.send(1)

    mine = pl.ds(pl.multiple_of(p.d * slab, slab), slab)

    def slab_z(k, t):
        return remote(ow.at[mine], outw.at[z, mine], ss_wz.at[k], rs_wz.at[z], p.along(t))

    for k, t in enumerate(others):
        slab_z(k, t).start()
    outw[pl.ds(z, 1), mine] = ow[mine, :][None]
    slabs = Plane(p, lambda who: outw.at[:, pl.ds(who * slab, slab)], ss_wp, rs_wp)
    dy[pl.ds(p.d, 1)] = cot[...][None]
    grads = Plane(p, lambda who: dy.at[who], ss_cot, rs_cot)
    grads.send()

    def project(s):
        for t in range(3):
            part = mm(first[pl.ds(s, 1)][0], wq[t]) + bq[t : t + 1, :]
            mixed[pl.ds(pl.multiple_of(s * rows, rows), rows), t * share : (t + 1) * share] = part.astype(BF)

    project(z)
    for k in (1, 2):
        project(line.take(k))
    for t in others:
        remote(outw.at[t, mine], outw.at[t, mine], ss_wz.at[0], rs_wz.at[t], p.along(z)).wait_recv()
    slabs.send()

    mine_part = pl.ds(pl.multiple_of(p.d * part, part), part)

    def up_view(s):
        return up.at[:, pl.ds(pl.multiple_of(s * part, part), part)]

    def down_view(s):
        return down.at[pl.ds(pl.multiple_of(s * part, part), part)]

    def up_copy(k, s, t):
        return remote(upw.at[:, mine_part], up_view(s), ss_up.at[k], rs_up.at[s], p.along(t))

    def down_copy(k, s, t):
        return remote(dww.at[mine_part], down_view(s), ss_dn.at[k], rs_dn.at[s], p.along(t))

    def bias_copy(k, s, t):
        return remote(upb.at[p.d], ub.at[s], ss_ub.at[k], rs_ub.at[s], p.along(t))

    local_in = [
        pltpu.make_async_copy(upw.at[:, mine_part], up_view(z), sem_in.at[0]),
        pltpu.make_async_copy(dww.at[mine_part], down_view(z), sem_in.at[1]),
        pltpu.make_async_copy(upb.at[p.d], ub.at[z], sem_in.at[2]),
    ]
    for copy in local_in:
        copy.start()
    for k, t in enumerate(others):
        bias_copy(k, z, t).start()
        up_copy(k, z, t).start()
    project(line.take(3))

    def ctx_send(r):
        return remote(own.at[r], ctx.at[z], ss_ctx.at[r], rs_ctx.at[z], p.along(r))

    for r in reversed(range(4)):
        for h in range(heads):
            scores = softmax_block(mixed, h, r, share, rows, segc, segr, factor)
            peak = jnp.max(scores, -1, keepdims=True)
            expo = jnp.exp(scores - peak)
            total = jnp.sum(expo, -1, keepdims=True)
            probs = (expo / total).astype(BF)
            v = mixed[0 : (r + 1) * rows, 2 * share + h * HD : 2 * share + (h + 1) * HD]
            own[r, :, h * HD : (h + 1) * HD] = mm(probs, v).astype(BF)
            lse[h, r * rows : (r + 1) * rows, :] = jnp.broadcast_to(peak + jnp.log(total), (rows, HD))

        @pl.when(z != r)
        def _():
            ctx_send(r).start()

        @pl.when(z == r)
        def _():
            ctx[r] = own[r]

        if r == 3:
            for i in (1, 2, 3):
                slabs.take(i)
        if r == 2:
            for i in (1, 2, 3):
                grads.take(i)
    for k, t in enumerate(others):
        down_copy(k, z, t).start()
    outs = [
        pltpu.make_async_copy(a, b, sem_out.at[i])
        for i, (a, b) in enumerate(((first, first_out), (mixed, mixed_out), (own, own_out), (lse, lse_out)))
    ]
    for copy in outs:
        copy.start()
    slabs.take(0)
    for i in (1, 2, 3):
        slabs.take_second(i)
    attended = mm(ctx[pl.ds(z, 1)][0], outw[pl.ds(z, 1)][0])
    for t in others:
        remote(own.at[0], ctx.at[t], ss_ctx.at[0], rs_ctx.at[t], p.along(z)).wait_recv()
        attended = attended + mm(ctx[pl.ds(t, 1)][0], outw[pl.ds(t, 1)][0])
    middle = x_ref[...].astype(F32) + (attended + ob[...])
    dmid_out[...] = middle
    normed, _ = norm(middle)
    second[pl.ds(p.d, 1)] = (normed * g2[...] + b2[...]).astype(BF)[None]
    seconds = Plane(p, lambda who: second.at[who], ss_sec, rs_sec)
    seconds.send()

    grads.take(0)
    for i in (1, 2, 3):
        grads.take_second(i)
    for copy in local_in:
        copy.wait()
    for k, t in enumerate(others):
        bias_copy(k, t, z).wait_recv()
        up_copy(k, t, z).wait_recv()
        down_copy(k, t, z).wait_recv()
    up_bias = jnp.concatenate([ub[q] for q in range(4)], 1)

    def give(parts, got, ss, rs, i):
        return remote(parts.at[i, 1 - p.core], got.at[i], ss.at[i], rs.at[i], p.plane(p.sibling))

    def ship(sums, into, ss, rs, i):
        return remote(sums.at[i - 1], into.at[i - 1], ss.at[i - 1], rs.at[i - 1], p.plane(p.chip(i)))

    def summed(parts, got, i):
        return parts[pl.ds(i, 1), pl.ds(p.core, 1)][0, 0].astype(F32) + got[pl.ds(i, 1)][0].astype(F32)

    def feed(i, carry):
        @pl.when(i == 0)
        def _():
            seconds.take(0)

        @pl.when(i > 0)
        def _():
            who = p.chip(i)
            seconds_take(i)
            other = who + p.sibling - p.d
            seconds._second(i, other).wait_recv()

        pair = pl.ds(p.chip(i) - p.core, 2)
        tokens = second[pair].reshape(2 * rows, width)
        pre = mm(tokens, up[...]) + up_bias
        value, slope = gelu_parts(pre)
        value = value.astype(BF)
        hidden[pair] = value.reshape(2, rows, 4 * part)
        back = mm_nt(dy[pair].reshape(2 * rows, width), down[...])
        back = (back * slope).astype(BF)
        dpre[pair] = back.reshape(2, rows, 4 * part)
        ds_part[pl.ds(i, 1)] = mm_nt(back, up[...]).astype(BF).reshape(1, 2, rows, width)
        give(ds_part, ds_got, ss_ds, rs_ds, i).start()
        o_part[pl.ds(i, 1)] = mm(value, down[...]).astype(BF).reshape(1, 2, rows, width)
        give(o_part, o_got, ss_do, rs_do, i).start()
        give(ds_part, ds_got, ss_ds, rs_ds, i).wait_recv()

        @pl.when(i > 0)
        def _():
            ds_sum[pl.ds(i - 1, 1)] = summed(ds_part, ds_got, i).astype(BF)[None]
            ship(ds_sum, ds_in, ss_og, rs_og, i).start()

        return carry

    def seconds_take(i):
        who = p.chip(i)
        remote(second.at[who], second.at[who], ss_sec.at[i], rs_sec.at[i], p.plane(p.d)).wait_recv()
        seconds._second(i, who).start()

    lax.fori_loop(0, 4, feed, 0)
    for i in range(4):
        give(o_part, o_got, ss_do, rs_do, i).wait_recv()
        if i:
            o_sum[i - 1] = summed(o_part, o_got, i).astype(BF)
            ship(o_sum, o_in, ss_oo, rs_oo, i).start()

    def quarter(q):
        return pl.ds(pl.multiple_of(q * part, part), part)

    def dg_copy(k, s, t):
        return remote(dg.at[quarter(t)], dg_in.at[k], ss_dg.at[k], rs_dg.at[k], p.along(t))

    all_dy = dy[...].reshape(8 * rows, width)
    for c in range(2):
        cols = slice(c * 2 * part, (c + 1) * 2 * part)
        dg[cols, :] = mm_tn(hidden[:, :, cols].reshape(8 * rows, 2 * part), all_dy).astype(BF)
    for k, t in enumerate(others):
        dg_copy(k, z, t).start()

    total = summed(ds_part, ds_got, 0)
    for i in (1, 2, 3):
        ship(ds_sum, ds_in, ss_og, rs_og, i).wait_recv()
        total = total + ds_in[i - 1].astype(F32)
    middle = dmid_out[...]
    normed, scale = norm(middle)
    grad = cot[...].astype(F32)
    scaled = total * g2[...]
    dmiddle = grad + scale * (
        scaled - jnp.mean(scaled, -1, keepdims=True) - normed * jnp.mean(scaled * normed, -1, keepdims=True)
    )
    low = dmiddle.astype(BF)
    for t in range(4):
        dcs[t] = mm_nt(low, outw[t]).astype(BF)

    def dc_copy(k, t):
        return remote(dcs.at[t], dctx.at[z], ss_dc.at[k], rs_dc.at[z], p.along(t))

    for k, t in enumerate(others):
        dc_copy(k, t).start()
    dctx[pl.ds(z, 1)] = dcs[pl.ds(z, 1)]
    small_out[...] = jnp.concatenate(
        [
            jnp.sum(total * normed, 0, keepdims=True), jnp.sum(total, 0, keepdims=True),
            jnp.sum(low.astype(F32), 0, keepdims=True), jnp.sum(grad, 0, keepdims=True),
            jnp.zeros((4, width), F32),
        ],
        0,
    )
    for t in range(4):
        owg[t] = mm_tn(ctx[t], low).astype(BF)
    all_dpre = dpre[...].reshape(8 * rows, 4 * part)
    ubg_out[...] = jnp.sum(all_dpre.astype(F32), 0, keepdims=True)
    for c in range(4):
        cols = slice(c * width // 4, (c + 1) * width // 4)
        ug[cols, :] = mm_tn(second[:, :, cols].reshape(8 * rows, width // 4), all_dpre).astype(BF)
    late = [
        pltpu.make_async_copy(a, b, sem_out.at[4 + i])
        for i, (a, b) in enumerate(((ug, ug_out), (owg, owg_out)))
    ]
    for copy in late:
        copy.start()
    reduced = summed(o_part, o_got, 0)
    for i in (1, 2, 3):
        ship(o_sum, o_in, ss_oo, rs_oo, i).wait_recv()
        reduced = reduced + o_in[i - 1].astype(F32)
    output[...] = (middle + (reduced + dwb[...])).astype(BF)
    dmid_out[...] = dmiddle
    down_sum = dg[quarter(z), :].astype(F32)
    for k in range(3):
        dg_copy(k, z, z).wait_recv()
        down_sum = down_sum + dg_in[k].astype(F32)
    dg_out[...] = down_sum.astype(BF)
    for k, t in enumerate(others):
        remote(dcs.at[0], dctx.at[t], ss_dc.at[k], rs_dc.at[t], p.along(z)).wait_recv()
    last = pltpu.make_async_copy(dctx, dctx_out, sem_out.at[6])
    last.start()

    line.finish()
    slabs.finish()
    grads.finish()
    seconds.finish()
    for k, t in enumerate(others):
        slab_z(k, t).wait_send()
        bias_copy(k, z, t).wait_send()
        up_copy(k, z, t).wait_send()
        down_copy(k, z, t).wait_send()
        dg_copy(k, z, t).wait_send()
        dc_copy(k, t).wait_send()
    for r in range(4):

        @pl.when(z != r)
        def _():
            ctx_send(r).wait_send()

        give(ds_part, ds_got, ss_ds, rs_ds, r).wait_send()
        give(o_part, o_got, ss_do, rs_do, r).wait_send()
        if r:
            ship(ds_sum, ds_in, ss_og, rs_og, r).wait_send()
            ship(o_sum, o_in, ss_oo, rs_oo, r).wait_send()
    for copy in outs + late + [last]:
        copy.wait()


def run_front(x, cot, seg_ids, g1, b1, wq, bq, ow, ob, g2, b2, upw, upb, dww, dwb):
    rows, width = x.shape
    share = wq.shape[2]
    length = 4 * rows
    vm = pl.BlockSpec(memory_space=VMEM)
    hbm = pl.BlockSpec(memory_space=pl.ANY)
    heads = share // HD
    part = upw.shape[1] // 8
    outs = [
        (hbm, (4, rows, width), BF), (hbm, (length, 3 * share), BF), (hbm, (4, rows, share), BF),
        (hbm, (heads, length, HD), F32), (hbm, (4, rows, share), BF), (hbm, (width, 4 * part), BF),
        (hbm, (4, share, width), BF), (vm, (rows, width), BF), (vm, (rows, width), F32), (vm, (part, width), BF),
        (vm, (1, 4 * part), F32), (vm, (8, width), F32),
    ]
    token = (rows, width)
    return pl.pallas_call(
        front,
        out_shape=[jax.ShapeDtypeStruct(s, t) for _, s, t in outs],
        in_specs=[vm] * 12 + [hbm, vm, hbm, vm],
        out_specs=[m for m, _, _ in outs],
        scratch_shapes=[
            VMEM((4,) + token, BF), VMEM((length, 3 * share), BF), VMEM((4, rows, share), BF),
            VMEM((4, rows, share), BF), VMEM((4, share, width), BF), VMEM((heads, length, HD), F32),
            VMEM((width, 4 * part), BF), VMEM((4 * part, width), BF), VMEM((4, 1, part), F32),
            VMEM((8,) + token, BF), VMEM((8,) + token, BF), VMEM((8, rows, 4 * part), BF), VMEM((8, rows, 4 * part), BF),
            VMEM((4, 2) + token, BF), VMEM((4,) + token, BF), VMEM((3,) + token, BF), VMEM((3,) + token, BF),
            VMEM((4, 2) + token, BF), VMEM((4,) + token, BF), VMEM((3,) + token, BF), VMEM((3,) + token, BF),
            VMEM((4 * part, width), BF), VMEM((3, part, width), BF), VMEM((width, 4 * part), BF),
            VMEM((4, share, width), BF), VMEM((4, rows, share), BF), VMEM((4, rows, share), BF),
            DMA((5, 2)), DMA((4, 2)), DMA((4,)), DMA((4,)), DMA((3,)), DMA((4,)),
            DMA((7,)), DMA((7,)), DMA((7,)), DMA((7,)), DMA((3,)), DMA((4,)), DMA((3,)), DMA((4,)),
            DMA((3,)), DMA((4,)), DMA((7,)), DMA((7,)), DMA((3,)), DMA((3,)), DMA((4,)), DMA((4,)),
            DMA((4,)), DMA((4,)), DMA((3,)), DMA((3,)), DMA((3,)), DMA((3,)), DMA((3,)), DMA((4,)),
            DMA((7,)), DMA((3,)),
        ],
        compiler_params=pltpu.CompilerParams(collective_id=0, has_side_effects=True, vmem_limit_bytes=63 << 20),
        name="front",
    )(
        x, cot, seg_ids.reshape(1, length), seg_ids.reshape(length, 1), g1.reshape(1, width), b1.reshape(1, width),
        wq, bq, ow, ob.reshape(1, width), g2.reshape(1, width), b2.reshape(1, width),
        upw, upb.reshape(8, 1, part), dww, dwb.reshape(1, width),
    )


class PlaneSum:
    def __init__(self, place, view, got, sums, into, ss, rs):
        self.p, self.view, self.got, self.sums, self.into, self.ss, self.rs = place, view, got, sums, into, ss, rs

    def _give(self, i):
        p = self.p
        who = p.chip(i) + p.sibling - p.d
        return remote(self.view(who), self.got.at[i], self.ss.at[i], self.rs.at[i], p.plane(p.sibling))

    def _ship(self, i):
        p = self.p
        return remote(
            self.sums.at[i - 1], self.into.at[i - 1], self.ss.at[3 + i], self.rs.at[3 + i], p.plane(p.chip(i))
        )

    def give(self):
        for i in (1, 2, 3, 0):
            self._give(i).start()

    def _both(self, i):
        return self.view(self.p.chip(i))[...].astype(F32) + self.got[i].astype(F32)

    def ship(self):
        for i in (1, 2, 3):
            self._give(i).wait_recv()
            self.sums[i - 1] = self._both(i).astype(BF)
            self._ship(i).start()

    def total(self):
        self._give(0).wait_recv()
        total = self._both(0)
        for i in (1, 2, 3):
            self._ship(i).wait_recv()
            total = total + self.into[i - 1].astype(F32)
        return total

    def finish(self):
        for i in range(4):
            self._give(i).wait_send()
            if i:
                self._ship(i).wait_send()


def rear(
    first, mixed, own, lse, dctx, segr, segc, wq, x_ref, dmid, g1, ug, dg, owg, ubg, small,
    tokens_grad, small_out, pg_out, pb_out, owg_out, upg_out, ubg_out, dng_out,
    acc, dmixed, delta, parts, in_end, in_mid, fwd, pg, pg_got, pg_sum, pg_in, pga, pb, dga, uga, uba, oga,
    og_got, og_sum, og_in, ogz, ogz_in, ug_in, ub_in, sm, sm_in, smp, pg_f, owg_f, upg_f, dng_f,
    ss_dg, rs_dg, ss_og, rs_og, ss_oz, rs_oz, ss_oa, rs_oa, ss_ug, rs_ug, ss_ua, rs_ua, ss_ub, rs_ub, ss_ba, rs_ba,
    ss_pg, rs_pg, ss_pa, rs_pa, ss_pb, rs_pb, ss_end, rs_end, ss_mid, rs_mid, ss_sm, rs_sm, ss_sp, rs_sp, sem_out,
):
    p = Place()
    z = p.z
    rows, width = x_ref.shape
    share = wq.shape[2]
    heads = share // HD
    factor = 1.0 / math.sqrt(HD)
    slab = owg.shape[1] // 8
    part = dg.shape[0]
    line = width // 8
    others = [lax.rem(z + k, 4) for k in (1, 2, 3)]
    enter = barrier([p.along(t) for t in others] + [p.plane(p.chip(i)) for i in (1, 2, 3)] + [p.plane(p.sibling)])
    low_half = 1 - z // 2
    inner = lax.rem(z + 1, 4) // 2
    toward = z + 2 * low_half - 1
    outward = z + 1 - 2 * low_half

    for h in range(heads):
        cols = slice(h * HD, (h + 1) * HD)
        product = dctx[:, :, cols].astype(F32) * own[:, :, cols].astype(F32)
        delta[h] = jnp.broadcast_to(jnp.sum(product, -1, keepdims=True).reshape(4 * rows, 1), (4 * rows, HD))
    for t in range(3):
        acc[t] = jnp.zeros((4 * rows, share), F32)
    enter()

    down_all = Plane(p, lambda who: dga.at[who], ss_dg, rs_dg)
    dga[pl.ds(p.d, 1)] = dg[...][None]
    down_all.send()
    out_sum = PlaneSum(p, lambda who: owg.at[:, pl.ds(who * slab, slab)], og_got, og_sum, og_in, ss_og, rs_og)
    out_sum.give()

    def quarter(q):
        return pl.ds(pl.multiple_of(q * part, part), part)

    def ug_copy(k, t):
        return remote(ug.at[:, quarter(t)], ug_in.at[k], ss_ug.at[k], rs_ug.at[k], p.along(t))

    def ub_copy(k, t):
        return remote(ubg.at[t], ub_in.at[k], ss_ub.at[k], rs_ub.at[k], p.along(t))

    for k, t in enumerate(others):
        ub_copy(k, t).start()
        ug_copy(k, t).start()

    pieces = 4
    piece = rows // pieces

    def chunk(c):
        return pl.ds(c * piece, piece)

    def from_end(g, c):
        return remote(
            parts.at[g, chunk(c)], in_end.at[g, chunk(c)], ss_end.at[g, c], rs_end.at[g, c], p.along(toward)
        )

    def from_mid(g, c):
        return remote(
            fwd.at[g, chunk(c)], in_mid.at[g, chunk(c)], ss_mid.at[g, c], rs_mid.at[g, c], p.along(toward)
        )

    def to_end(c):
        return remote(fwd.at[2, chunk(c)], in_end.at[0, chunk(c)], ss_mid.at[2, c], rs_end.at[0, c], p.along(outward))

    def strip(index):
        return pl.ds(pl.multiple_of(index * rows, rows), rows)

    for g in range(4):

        def block(e, carry):
            i = (g + e) + low_half * (3 - g - (g + e))
            j = g + low_half * (3 - (g + e) - g)
            qs, ks = strip(i), strip(j)
            place_q = i * rows + lax.broadcasted_iota(jnp.int32, (rows, rows), 0)
            place_k = j * rows + lax.broadcasted_iota(jnp.int32, (rows, rows), 1)
            allowed = (segc[qs, :] == segr[:, ks]) & (place_q >= place_k)
            for h in range(heads):
                cols = slice(h * HD, (h + 1) * HD)
                q = mixed[qs, cols]
                k = mixed[ks, share + h * HD : share + (h + 1) * HD]
                v = mixed[ks, 2 * share + h * HD : 2 * share + (h + 1) * HD]
                up = dctx[pl.ds(i, 1), :, cols][0]
                scores = jnp.where(allowed, mm_nt(q, k) * factor, -1e30)
                probs = jnp.exp(scores - lse[h, qs, 0:1])
                acc[2, ks, cols] += mm_tn(probs.astype(BF), up)
                back = (probs * (mm_nt(up, v) - delta[h, qs, 0:1])).astype(BF)
                acc[0, qs, cols] += mm(back, k)
                acc[1, ks, cols] += mm_tn(back, q)
            return carry

        lax.fori_loop(0, 4 - g, block, 0)
        r = g + low_half * (3 - 2 * g)
        total = None
        for t in range(3):
            value = acc[t, strip(r), :]
            low = (value * factor if t < 2 else value).astype(BF)
            dmixed[strip(r), t * share : (t + 1) * share] = low
            term = mm_nt(low, wq[t])
            total = term if total is None else total + term
        parts[g] = total.astype(BF)
        if g < 3:

            @pl.when(inner == 0)
            def _():
                for c in range(pieces):
                    from_end(g, c).start()

        if g == 1:
            out_sum.ship()

    whole = first[...].reshape(4 * rows, width)
    for t in range(3):
        cols = slice(t * share, (t + 1) * share)
        pg[:, cols] = mm_tn(whole, dmixed[:, cols]).astype(BF)
    pb[pl.ds(p.d, 1)] = jnp.sum(dmixed[...].astype(F32), 0, keepdims=True)[None]
    pg_sums = PlaneSum(p, lambda who: pg.at[pl.ds(pl.multiple_of(who * line, line), line)], pg_got, pg_sum, pg_in, ss_pg, rs_pg)
    pg_sums.give()
    pb_all = Plane(p, lambda who: pb.at[who], ss_pb, rs_pb)
    pb_all.send()
    pg_sums.ship()

    @pl.when(inner == 1)
    def _():
        for c in range(pieces):
            from_end(0, c).wait_recv()
            fwd[0, chunk(c)] = (parts[0, chunk(c)].astype(F32) + in_end[0, chunk(c)].astype(F32)).astype(BF)
            from_mid(0, c).start()
        for c in range(pieces):
            from_mid(0, c).wait_recv()
            fwd[2, chunk(c)] = (parts[3, chunk(c)].astype(F32) + in_mid[0, chunk(c)].astype(F32)).astype(BF)
            to_end(c).start()

    og_total = out_sum.total().astype(BF)
    ogz[...] = og_total

    def oz_copy(k, t):
        return remote(ogz.at[t], ogz_in.at[k], ss_oz.at[k], rs_oz.at[k], p.along(t))

    for k, t in enumerate(others):
        oz_copy(k, t).start()
    for i in (1, 2, 3):
        down_all.take(i)
        pb_all.take(i)
    up_sum = ug[:, quarter(z)].astype(F32)
    ub_sum = ubg[pl.ds(z, 1)][0]
    for k, t in enumerate(others):
        ug_copy(k, t).wait_recv()
        ub_copy(k, t).wait_recv()
        up_sum = up_sum + ug_in[k].astype(F32)
        ub_sum = ub_sum + ub_in[k]
    uga[pl.ds(p.d, 1)] = up_sum.astype(BF)[None]
    uba[pl.ds(p.d, 1)] = ub_sum[None]
    up_all = Plane(p, lambda who: uga.at[who], ss_ua, rs_ua)
    ub_all = Plane(p, lambda who: uba.at[who], ss_ba, rs_ba)
    pg_all = Plane(p, lambda who: pga.at[who], ss_pa, rs_pa)
    pga[pl.ds(p.d, 1)] = pg_sums.total().astype(BF)[None]
    pg_all.send()
    up_all.send()
    ub_all.send()

    @pl.when(inner == 1)
    def _():
        for c in range(pieces):
            from_end(1, c).wait_recv()
            fwd[1, chunk(c)] = (parts[1, chunk(c)].astype(F32) + in_end[1, chunk(c)].astype(F32)).astype(BF)
            from_mid(1, c).start()

    down_all.take(0)
    pb_all.take(0)
    for i in (1, 2, 3):
        down_all.take_second(i)
        pb_all.take_second(i)
    for who in range(8):
        dng_f[who * part : (who + 1) * part, :] = dga[who].astype(F32)
    pb_out[...] = jnp.sum(pb[...], 0)
    out_copies = [pltpu.make_async_copy(dng_f, dng_out, sem_out.at[0])]
    out_copies[0].start()
    oz_sum = ogz[pl.ds(z, 1)][0].astype(F32)
    for k, t in enumerate(others):
        oz_copy(k, t).wait_recv()
        oz_sum = oz_sum + ogz_in[k].astype(F32)
    oga[pl.ds(p.d, 1)] = oz_sum.astype(BF)[None]
    og_all = Plane(p, lambda who: oga.at[who], ss_oa, rs_oa)
    og_all.send()
    block_x = x_ref[...].astype(F32)
    normed, scale = norm(block_x)
    for i in (1, 2, 3):
        pg_all.take(i)

    @pl.when(inner == 0)
    def _():
        for c in range(pieces):
            to_end(c).wait_recv()
        acc[0, 0:rows, :] = (parts[3, :, 0:share].astype(F32) + in_end[0, :, 0:share].astype(F32))
        acc[0, rows : 2 * rows, :] = parts[3, :, share : 2 * share].astype(F32) + in_end[0, :, share : 2 * share].astype(F32)
        acc[0, 2 * rows : 3 * rows, :] = (
            parts[3, :, 2 * share : 3 * share].astype(F32) + in_end[0, :, 2 * share : 3 * share].astype(F32)
        )
        acc[0, 3 * rows : 4 * rows, :] = parts[3, :, 3 * share :].astype(F32) + in_end[0, :, 3 * share :].astype(F32)

    @pl.when(inner == 1)
    def _():
        for c in range(pieces):
            from_end(2, c).wait_recv()
            from_mid(1, c).wait_recv()
        for n in range(4):
            cols = slice(n * share, (n + 1) * share)
            acc[0, n * rows : (n + 1) * rows, :] = (
                parts[2, :, cols].astype(F32) + in_end[2, :, cols].astype(F32) + in_mid[1, :, cols].astype(F32)
            )

    total = jnp.concatenate([acc[0, n * rows : (n + 1) * rows, :] for n in range(4)], 1)
    scaled = total * g1[...]
    back = scale * (
        scaled - jnp.mean(scaled, -1, keepdims=True) - normed * jnp.mean(scaled * normed, -1, keepdims=True)
    )
    tokens_grad[...] = (dmid[...] + back).astype(BF)
    sm[...] = jnp.concatenate(
        [
            small[0:4, :], jnp.sum(total * normed, 0, keepdims=True), jnp.sum(total, 0, keepdims=True),
            jnp.zeros((2, width), F32),
        ],
        0,
    )

    def sm_copy(k, t):
        return remote(sm, sm_in.at[k], ss_sm.at[k], rs_sm.at[k], p.along(t))

    for k, t in enumerate(others):
        sm_copy(k, t).start()
    for i in (1, 2, 3):
        up_all.take(i)
        ub_all.take(i)
        og_all.take(i)
    sm_sum = sm[...]
    for k, t in enumerate(others):
        sm_copy(k, t).wait_recv()
        sm_sum = sm_sum + sm_in[k]
    smp[pl.ds(p.d, 1)] = sm_sum[None]
    sm_all = Plane(p, lambda who: smp.at[who], ss_sp, rs_sp)
    sm_all.send()

    pg_all.take(0)
    for i in (1, 2, 3):
        pg_all.take_second(i)
    for t in range(3):
        for who in range(8):
            pg_f[t, who * line : (who + 1) * line, :] = pga[who, :, t * share : (t + 1) * share].astype(F32)
    out_copies.append(pltpu.make_async_copy(pg_f, pg_out, sem_out.at[1]))
    out_copies[-1].start()
    for i in (1, 2, 3):
        sm_all.take(i)
    up_all.take(0)
    ub_all.take(0)
    og_all.take(0)
    for i in (1, 2, 3):
        up_all.take_second(i)
        ub_all.take_second(i)
        og_all.take_second(i)
    for who in range(8):
        upg_f[:, who * part : (who + 1) * part] = uga[who].astype(F32)
        ubg_out[:, who * part : (who + 1) * part] = uba[who]
    out_copies.append(pltpu.make_async_copy(upg_f, upg_out, sem_out.at[2]))
    out_copies[-1].start()
    for who in range(8):
        owg_f[who * slab : (who + 1) * slab, :] = oga[who].astype(F32)
    out_copies.append(pltpu.make_async_copy(owg_f, owg_out, sem_out.at[3]))
    out_copies[-1].start()
    sm_all.take(0)
    for i in (1, 2, 3):
        sm_all.take_second(i)
    small_out[...] = jnp.sum(smp[...], 0)

    for group in (down_all, out_sum, pg_sums, pb_all, up_all, ub_all, pg_all, og_all, sm_all):
        group.finish()
    for k, t in enumerate(others):
        ug_copy(k, t).wait_send()
        ub_copy(k, t).wait_send()
        oz_copy(k, t).wait_send()
        sm_copy(k, t).wait_send()

    @pl.when(inner == 0)
    def _():
        for g in range(3):
            for c in range(pieces):
                from_end(g, c).wait_send()

    @pl.when(inner == 1)
    def _():
        for c in range(pieces):
            from_mid(0, c).wait_send()
            from_mid(1, c).wait_send()
            to_end(c).wait_send()

    for copy in out_copies:
        copy.wait()


def run_rear(first, mixed, own, lse, dctx, seg_ids, wq, x, dmid, g1, ug, dg, owg, ubg, small):
    rows, width = x.shape
    share = wq.shape[2]
    length = 4 * rows
    heads = share // HD
    part = dg.shape[0]
    slab = share // 8
    line = width // 8
    vm = pl.BlockSpec(memory_space=VMEM)
    hbm = pl.BlockSpec(memory_space=pl.ANY)
    outs = [
        (vm, (rows, width), BF), (vm, (8, width), F32), (hbm, (3, width, share), F32), (vm, (1, 3 * share), F32),
        (hbm, (share, width), F32), (hbm, (width, 8 * part), F32), (vm, (1, 8 * part), F32), (hbm, (8 * part, width), F32),
    ]
    token = (rows, width)
    seven = [DMA((7,)), DMA((7,))]
    three = [DMA((3,)), DMA((3,))]
    return pl.pallas_call(
        rear,
        out_shape=[jax.ShapeDtypeStruct(s, t) for _, s, t in outs],
        in_specs=[vm] * 16,
        out_specs=[m for m, _, _ in outs],
        scratch_shapes=[
            VMEM((3, length, share), F32), VMEM((length, 3 * share), BF), VMEM((heads, length, HD), F32),
            VMEM((4,) + token, BF), VMEM((3,) + token, BF), VMEM((2,) + token, BF), VMEM((3,) + token, BF),
            VMEM((width, 3 * share), BF), VMEM((4, line, 3 * share), BF), VMEM((3, line, 3 * share), BF),
            VMEM((3, line, 3 * share), BF), VMEM((8, line, 3 * share), BF), VMEM((8, 1, 3 * share), F32),
            VMEM((8, part, width), BF), VMEM((8, width, part), BF), VMEM((8, 1, part), F32), VMEM((8, slab, width), BF),
            VMEM((4, 4, slab, width), BF), VMEM((3, 4, slab, width), BF), VMEM((3, 4, slab, width), BF),
            VMEM((4, slab, width), BF), VMEM((3, slab, width), BF), VMEM((3, width, part), BF), VMEM((3, 1, part), F32),
            VMEM((8, width), F32), VMEM((3, 8, width), F32), VMEM((8, 8, width), F32),
            VMEM((3, width, share), F32), VMEM((share, width), F32), VMEM((width, 8 * part), F32), VMEM((8 * part, width), F32),
        ]
        + seven + seven + three + seven + three + seven + three + seven
        + seven + seven + seven + [DMA((3, 4)), DMA((3, 4)), DMA((3, 4)), DMA((2, 4))] + three + seven + [DMA((4,))],
        compiler_params=pltpu.CompilerParams(collective_id=1, has_side_effects=True, vmem_limit_bytes=63 << 20),
        name="rear",
    )(
        first, mixed, own, lse, dctx, seg_ids.reshape(1, length), seg_ids.reshape(length, 1), wq, x, dmid,
        g1.reshape(1, width), ug, dg, owg, ubg.reshape(4, 1, part), small,
    )


def shards(
    tokens, seg_ids, cotangent, first_gain, first_shift, project_weight, project_bias, out_weight, out_bias,
    second_gain, second_shift, up_weight, up_bias, down_weight, down_bias,
):
    first, mixed, own, lse, dctx, ug, owg, output, dmid, dg, ubg, small = run_front(
        tokens, cotangent, seg_ids, first_gain, first_shift, project_weight, project_bias, out_weight, out_bias,
        second_gain, second_shift, up_weight, up_bias, down_weight, down_bias,
    )
    tokens_grad, sums, project_grad, pbias_grad, outw_grad, up_grad, upbias_grad, down_grad = run_rear(
        first, mixed, own, lse, dctx, seg_ids, project_weight, tokens, dmid, first_gain, ug, dg, owg, ubg, small
    )
    pbias_grad = pbias_grad.reshape(project_bias.shape)
    upbias_grad = upbias_grad.reshape(up_bias.shape)
    reduced = (sums, project_grad, pbias_grad, outw_grad, up_grad, upbias_grad, down_grad)
    if lax.axis_size("dp") > 8:
        reduced = jax.tree.map(lambda v: v * 0.125, lax.psum(reduced, "dp"))
    sums, project_grad, pbias_grad, outw_grad, up_grad, upbias_grad, down_grad = reduced
    return (
        output, tokens_grad, sums[4], sums[5], project_grad, pbias_grad, outw_grad, sums[2], sums[0], sums[1],
        up_grad, upbias_grad, down_grad, sums[3],
    )


def solution(mesh):
    in_specs = (
        P(("dp", "mp"), None),
        P("dp"),
        P(("dp", "mp"), None),
        P(),
        P(),
        P(None, None, "mp"),
        P(None, "mp"),
        P("mp", None),
        P(),
        P(),
        P(),
        P(None, "mp"),
        P("mp"),
        P("mp", None),
        P(),
    )
    out_specs = (
        P(("dp", "mp"), None),
        P(("dp", "mp"), None),
        P(),
        P(),
        P(None, None, "mp"),
        P(None, "mp"),
        P("mp", None),
        P(),
        P(),
        P(),
        P(None, "mp"),
        P("mp"),
        P("mp", None),
        P(),
    )
    return jax.shard_map(shards, mesh=mesh, in_specs=in_specs, out_specs=out_specs, check_vma=False)
```

```python
import math

import jax
import jax.numpy as jnp
from jax import lax
from jax.experimental import pallas as pl
from jax.experimental.pallas import tpu as pltpu
from jax.sharding import PartitionSpec as P

HD = 128
EPS = 1e-05
BF = jnp.bfloat16
F32 = jnp.float32
MESH = pl.DeviceIdType.MESH
VMEM = pltpu.VMEM
DMA = pltpu.SemaphoreType.DMA
GELU_A = 0.7978845608
GELU_B = 0.044715


def mm(left, right):
    return jnp.dot(left, right, preferred_element_type=F32)


def mm_nt(left, right):
    return lax.dot_general(left, right, (((1,), (1,)), ((), ())), preferred_element_type=F32)


def mm_tn(left, right):
    return lax.dot_general(left, right, (((0,), (0,)), ((), ())), preferred_element_type=F32)


def remote(src, dst, ss, rs, device):
    return pltpu.make_async_remote_copy(
        src_ref=src, dst_ref=dst, send_sem=ss, recv_sem=rs, device_id=device, device_id_type=MESH
    )


def local(src, dst, sem):
    return pltpu.make_async_copy(src, dst, sem)


def barrier(devices):
    sem = pltpu.get_barrier_semaphore()
    for device in devices:
        pl.semaphore_signal(sem, 1, device_id=device, device_id_type=MESH)
    return lambda: pl.semaphore_wait(sem, len(devices))


def start(copy):
    copy.start()


def wait(copy):
    copy.wait()


def sent(copy):
    copy.wait_send()


def came(copy):
    copy.wait_recv()


def norm(values):
    mean = jnp.mean(values, -1, keepdims=True)
    centered = values - mean
    var = jnp.mean(centered * centered, -1, keepdims=True)
    scale = lax.rsqrt(var + EPS)
    return centered * scale, scale


def norm_back(grad, normed, scale, gain):
    scaled = grad * gain
    return scale * (
        scaled - jnp.mean(scaled, -1, keepdims=True) - normed * jnp.mean(scaled * normed, -1, keepdims=True)
    )


def gelu_parts(v):
    square = v * v
    t = jnp.tanh(GELU_A * v * (1.0 + GELU_B * square))
    half = 0.5 * (1.0 + t)
    slope = half + 0.5 * v * (1.0 - t * t) * (GELU_A * (1.0 + 3.0 * GELU_B * square))
    return v * half, slope


class Place:
    def __init__(self):
        self.z = lax.axis_index("mp")
        self.dp = lax.axis_index("dp")
        self.d = lax.rem(self.dp, 8)
        self.base = self.dp - self.d
        self.core = lax.rem(self.d, 2)
        self.column = self.d // 2
        bit_x = lax.rem(self.column, 2)
        bit_y = self.column // 2
        self.step_x = 1 - 2 * bit_x
        self.step_y = 2 - 4 * bit_y
        self.sibling = self.dp + 1 - 2 * self.core
        self.swapped = lax.rem(self.core + self.z // 2, 2)
        self.far = lax.rem(self.z + 2, 4)
        self.rank = lax.rem(self.z + 2 * self.swapped, 4)
        self.odd = lax.rem(self.z, 2)

    def column_at(self, i):
        return self.column + (i % 2) * self.step_x + (i // 2) * self.step_y

    def chip(self, i):
        return {"dp": self.base + 2 * self.column_at(i) + self.core, "mp": self.z}

    def along(self, z):
        return {"dp": self.dp, "mp": z}

    def to_sibling(self):
        return {"dp": self.sibling, "mp": self.z}

    def across(self):
        return {"dp": self.dp, "mp": self.z + 1 - 2 * self.odd}

    def partner(self):
        return {"dp": self.sibling, "mp": self.far}

    def rank_of(self, k):
        return lax.rem(self.rank + (k // 2) * (1 - 2 * self.odd) + 2 * (k % 2), 4)

    def at_home(self, body):
        pl.when(self.swapped == 0)(body)

    def if_swapped(self, body):
        pl.when(self.swapped == 1)(body)


class Gather:
    def __init__(self, p, buf, ss, rs):
        self.p, self.buf, self.ss, self.rs = p, buf, ss, rs

    def _copy(self, k, i, device):
        view = self.buf.at[self.p.rank_of(k)]
        return remote(view, view, self.ss.at[i], self.rs.at[i], device)

    def send(self):
        self._copy(0, 0, self.p.across()).start()
        self._copy(0, 1, self.p.to_sibling()).start()

    def take(self):
        self._copy(2, 0, self.p.across()).wait_recv()
        self._copy(2, 2, self.p.to_sibling()).start()

    def near(self):
        self._copy(1, 1, self.p.to_sibling()).wait_recv()

    def last(self):
        self._copy(3, 2, self.p.to_sibling()).wait_recv()

    def finish(self):
        self._copy(0, 0, self.p.across()).wait_send()
        self._copy(0, 1, self.p.to_sibling()).wait_send()
        self._copy(2, 2, self.p.to_sibling()).wait_send()


class Sum:
    def __init__(self, p, parts, got, out, into, ss, rs):
        self.p, self.parts, self.got, self.out, self.into, self.ss, self.rs = p, parts, got, out, into, ss, rs

    def _give(self, n):
        k = 1 + 2 * n
        return remote(
            self.parts.at[self.p.rank_of(k)], self.got.at[n], self.ss.at[n], self.rs.at[n], self.p.to_sibling()
        )

    def _ship(self):
        return remote(self.out, self.into, self.ss.at[2], self.rs.at[2], self.p.across())

    def _part(self, k):
        return self.parts[pl.ds(self.p.rank_of(k), 1)][0].astype(F32)

    def give_far(self):
        self._give(1).start()

    def give_near(self):
        self._give(0).start()

    def ship(self):
        self._give(1).wait_recv()
        self.out[...] = (self._part(2) + self.got[1].astype(F32)).astype(BF)
        self._ship().start()

    def total(self):
        self._give(0).wait_recv()
        total = self._part(0) + self.got[0].astype(F32)
        self._ship().wait_recv()
        return total + self.into[...].astype(F32)

    def finish(self):
        self._give(0).wait_send()
        self._give(1).wait_send()
        self._ship().wait_send()


class Weight:
    def __init__(self, p, src, buf, part, ss, rs):
        self.p, self.src, self.buf, self.part, self.ss, self.rs = p, src, buf, part, ss, rs

    def _own(self):
        return local(self.src, self.buf, self.ss.at[0])

    def _swap(self):
        column = self.p.column
        return remote(self.part(self.src, column), self.part(self.buf, column), self.ss.at[0], self.rs.at[0], self.p.partner())

    def _share(self, i, column):
        view = self.part(self.buf, column)
        return remote(view, view, self.ss.at[i], self.rs.at[i], self.p.chip(i))

    def home(self):
        self._own().start()

    def swap(self):
        self._swap().start()

    def take(self):
        self._swap().wait_recv()
        for i in (1, 2, 3):
            self._share(i, self.p.column).start()

    def ready(self):
        self.p.at_home(lambda: self._own().wait())

        @self.p.if_swapped
        def _():
            for i in (1, 2, 3):
                self._share(i, self.p.column_at(i)).wait_recv()

    def finish(self):
        self._swap().wait_send()
        for i in (1, 2, 3):
            self._share(i, self.p.column).wait_send()


class Grad:
    def __init__(self, p, buf, part, into, total, far, out, ss, rs):
        self.p, self.buf, self.part, self.into, self.sum, self.far, self.out = p, buf, part, into, total, far, out
        self.ss, self.rs = ss, rs

    def _scatter(self, i):
        view = self.part(self.buf, self.p.column_at(i))
        return remote(view, self.into.at[i - 1], self.ss.at[i], self.rs.at[i], self.p.chip(i))

    def _home(self):
        return remote(self.sum, self.far, self.ss.at[0], self.rs.at[0], self.p.along(self.p.far))

    def _spread(self, i):
        view = self.part(self.out, self.p.column)
        device = self.p.chip(i) if i else self.p.to_sibling()
        return remote(self.sum, view, self.ss.at[4 + i], self.rs.at[4 + i], device)

    def _arrived(self, i):
        view = self.part(self.out, self.p.column_at(i))
        return remote(self.sum, view, self.ss.at[4 + i], self.rs.at[4 + i], self.p.chip(i))

    def _relay(self, i):
        view = self.part(self.out, self.p.column_at(i))
        return remote(view, view, self.ss.at[7 + i], self.rs.at[7 + i], self.p.to_sibling())

    def _keep(self):
        return local(self.sum, self.part(self.out, self.p.column), self.ss.at[11])

    def scatter(self):
        for i in (1, 2, 3):
            self._scatter(i).start()

    def combine(self):
        total = self.part(self.buf, self.p.column)[...].astype(F32)
        for i in (1, 2, 3):
            self._scatter(i).wait_recv()
            total = total + self.into[i - 1].astype(F32)
        self.sum[...] = total.astype(BF)
        self.p.if_swapped(lambda: self._home().start())

    def final(self):
        self._home().wait_recv()
        self.sum[...] = (self.sum[...].astype(F32) + self.far[...].astype(F32)).astype(BF)
        for i in (1, 2, 3, 0):
            self._spread(i).start()
        self._keep().start()

    def relay(self):
        for i in (1, 2, 3):
            self._arrived(i).wait_recv()
            self._relay(i).start()

    def finish(self):
        for i in (1, 2, 3):
            self._scatter(i).wait_send()

        @self.p.at_home
        def _():
            for i in range(4):
                self._spread(i).wait_send()
                if i:
                    self._relay(i).wait_send()
            self._keep().wait()

        @self.p.if_swapped
        def _():
            self._home().wait_send()
            self._spread(0).wait_recv()
            for i in (1, 2, 3):
                self._relay(i).wait_recv()


class Plane:
    def __init__(self, p, buf, ss, rs):
        self.p, self.buf, self.ss, self.rs = p, buf, ss, rs

    def _copy(self, column, core, i, device):
        view = self.buf.at[2 * column + core]
        return remote(view, view, self.ss.at[i], self.rs.at[i], device)

    def send(self):
        p = self.p
        for i in (1, 2, 3):
            self._copy(p.column, p.core, i, p.chip(i)).start()
        self._copy(p.column, p.core, 0, p.to_sibling()).start()

    def take(self):
        p = self.p
        for i in (1, 2, 3):
            self._copy(p.column_at(i), p.core, i, p.chip(i)).wait_recv()
            self._copy(p.column_at(i), p.core, 3 + i, p.to_sibling()).start()

    def rest(self):
        p = self.p
        self._copy(p.column, 1 - p.core, 0, p.to_sibling()).wait_recv()
        for i in (1, 2, 3):
            self._copy(p.column_at(i), 1 - p.core, 3 + i, p.to_sibling()).wait_recv()

    def finish(self):
        p = self.p
        self._copy(p.column, p.core, 0, p.to_sibling()).wait_send()
        for i in (1, 2, 3):
            self._copy(p.column, p.core, i, p.chip(i)).wait_send()
            self._copy(p.column_at(i), p.core, 3 + i, p.to_sibling()).wait_send()


def layer(
    x_ref, cot, seg_ref, g1, b1, wq_ref, bq_ref, ow_ref, ob, g2, b2, up_ref, ub_ref, dn_ref, dwb,
    output, tokens_grad, small_out, pg_out, og_out, ug_out, dg_out,
    xs, seg, segc, first, second, dy, dmid, mixed, own, stats, wq, bq, ow, up, ub, dn,
    a_part, a_got, a_out, a_in, s_part, s_got, s_out, s_in, o_part, o_got, o_out, o_in, f_got, f_out, f_in,
    hidden, dpre, dg, ug, pg, og, dg_in, ug_in, pg_in, og_in, dg_sum, ug_sum, pg_sum, og_sum,
    dg_far, ug_far, pg_far, og_far, acc, middle, dmiddle, rows_out, sm, sm_in, smp,
    ss_in, rs_in, ss_first, rs_first, ss_second, rs_second, ss_dy, rs_dy, ss_dmid, rs_dmid,
    ss_a, rs_a, ss_s, rs_s, ss_o, rs_o, ss_f, rs_f, ss_wq, rs_wq, ss_ow, rs_ow, ss_up, rs_up, ss_dn, rs_dn,
    ss_dg, rs_dg, ss_ug, rs_ug, ss_pg, rs_pg, ss_og, rs_og, ss_sm, rs_sm, ss_sp, rs_sp,
):
    p = Place()
    rows, width = xs.shape
    share = wq.shape[2]
    heads = share // HD
    factor = 1.0 / math.sqrt(HD)
    length = 4 * rows
    others = [lax.rem(p.z + k, 4) for k in (1, 2, 3)]
    enter = barrier([p.to_sibling(), p.partner()] + [p.along(t) for t in others] + [p.chip(i) for i in (1, 2, 3)])
    rank = p.rank

    def strip(index):
        return pl.ds(pl.multiple_of(index * rows, rows), rows)

    def piece(count, axis):
        def view(ref, column):
            size = ref.shape[axis] // count
            cut = pl.ds(pl.multiple_of(column * size, size), size)
            return ref.at[:, cut] if axis else ref.at[cut]

        return view

    by_rows, by_second = piece(4, 0), piece(4, 1)
    wq_move = Weight(p, wq_ref, wq, by_second, ss_wq, rs_wq)
    ow_move = Weight(p, ow_ref, ow, by_rows, ss_ow, rs_ow)
    up_move = Weight(p, up_ref, up, by_rows, ss_up, rs_up)
    dn_move = Weight(p, dn_ref, dn, by_rows, ss_dn, rs_dn)
    first_all = Gather(p, first, ss_first, rs_first)
    second_all = Gather(p, second, ss_second, rs_second)
    dy_all = Gather(p, dy, ss_dy, rs_dy)
    dmid_all = Gather(p, dmid, ss_dmid, rs_dmid)
    a_sum = Sum(p, a_part, a_got, a_out, a_in, ss_a, rs_a)
    s_sum = Sum(p, s_part, s_got, s_out, s_in, ss_s, rs_s)
    o_sum = Sum(p, o_part, o_got, o_out, o_in, ss_o, rs_o)
    f_sum = Sum(p, a_part, f_got, f_out, f_in, ss_f, rs_f)
    dn_grad = Grad(p, dg, by_rows, dg_in, dg_sum, dg_far, dg_out, ss_dg, rs_dg)
    up_grad = Grad(p, ug, by_rows, ug_in, ug_sum, ug_far, ug_out, ss_ug, rs_ug)
    pj_grad = Grad(p, pg, by_second, pg_in, pg_sum, pg_far, pg_out, ss_pg, rs_pg)
    ow_grad = Grad(p, og, by_rows, og_in, og_sum, og_far, og_out, ss_og, rs_og)

    def x_home():
        return local(x_ref, xs, ss_in.at[0])

    def cot_home():
        return local(cot, dy.at[rank], ss_in.at[1])

    def x_swap():
        return remote(x_ref, xs, ss_in.at[0], rs_in.at[0], p.partner())

    def cot_swap(slot):
        return remote(cot, dy.at[slot], ss_in.at[1], rs_in.at[1], p.partner())

    def bq_swap():
        return remote(bq_ref, bq, ss_in.at[2], rs_in.at[2], p.partner())

    def ub_swap():
        return remote(ub_ref, ub, ss_in.at[3], rs_in.at[3], p.partner())

    def seg_give():
        return remote(seg_ref, seg, ss_in.at[4], rs_in.at[4], p.to_sibling())

    def tg_back():
        return remote(rows_out.at[0], tokens_grad, ss_in.at[5], rs_in.at[5], p.partner())

    def out_back():
        return remote(rows_out.at[1], output, ss_in.at[6], rs_in.at[6], p.partner())

    def tg_home():
        return local(rows_out.at[0], tokens_grad, ss_in.at[5])

    def out_home():
        return local(rows_out.at[1], output, ss_in.at[6])

    @p.at_home
    def _():
        x_home().start()
        cot_home().start()
        for move in (wq_move, ow_move, up_move, dn_move):
            move.home()
        bq[...] = bq_ref[...]
        ub[...] = ub_ref[...]
        seg[...] = seg_ref[...]

    enter()

    @p.if_swapped
    def _():
        x_swap().start()
        wq_move.swap()
        bq_swap().start()
        ub_swap().start()

    @p.at_home
    def _():
        seg_give().start()
        x_home().wait()

    p.if_swapped(lambda: x_swap().wait_recv())
    normed, _ = norm(xs[...].astype(F32))
    first[pl.ds(rank, 1)] = (normed * g1[...] + b1[...]).astype(BF)[None]
    first_all.send()

    @p.if_swapped
    def _():
        wq_move.take()
        ow_move.swap()
        up_move.swap()
        seg_give().wait_recv()
        bq_swap().wait_recv()
        ub_swap().wait_recv()

    segc[...] = jnp.transpose(jnp.broadcast_to(seg[0:1, :], (HD, length)))

    def project(k):
        s = p.rank_of(k)
        block = first[pl.ds(s, 1)][0]
        for t in range(3):
            value = mm(block, wq[t]) + bq[t : t + 1, :]
            mixed[strip(s), t * share : (t + 1) * share] = value.astype(BF)

    @p.at_home
    def _():
        wq_move.ready()
        project(0)

    first_all.take()

    @p.at_home
    def _():
        cot_home().wait()
        dy_all.send()
        project(2)

    @p.if_swapped
    def _():
        ow_move.take()
        cot_swap(p.z).start()
        dn_move.swap()
        wq_move.ready()
        project(0)
        project(2)

    first_all.near()
    project(1)
    first_all.last()
    project(3)

    for r in reversed(range(4)):
        span = (r + 1) * rows
        top = r * rows
        place_q = top + lax.broadcasted_iota(jnp.int32, (rows, span), 0)
        place_k = lax.broadcasted_iota(jnp.int32, (rows, span), 1)
        allowed = (segc[top : top + rows, 0:1] == seg[0:1, 0:span]) & (place_q >= place_k)
        for h in range(heads):
            q = mixed[top : top + rows, h * HD : (h + 1) * HD]
            k = mixed[0:span, share + h * HD : share + (h + 1) * HD]
            v = mixed[0:span, 2 * share + h * HD : 2 * share + (h + 1) * HD]
            scores = jnp.where(allowed, mm_nt(q, k) * factor, -1e30)
            peak = jnp.max(scores, -1, keepdims=True)
            expo = jnp.exp(scores - peak)
            total = jnp.sum(expo, -1, keepdims=True)
            probs = (expo / total).astype(BF)
            own[r, :, h * HD : (h + 1) * HD] = mm(probs, v).astype(BF)
            stats[h, top : top + rows, 0:1] = peak + jnp.log(total)
    ow_move.ready()
    for r in range(4):
        a_part[r] = mm(own[r], ow[...]).astype(BF)
    a_sum.give_far()
    a_sum.give_near()
    a_sum.ship()

    @p.if_swapped
    def _():
        up_move.take()
        cot_swap(rank).wait_recv()
        dy_all.send()
        dn_move.take()

    dy_all.take()
    middle[...] = xs[...].astype(F32) + (a_sum.total() + ob[...])
    normed, _ = norm(middle[...])
    second[pl.ds(rank, 1)] = (normed * g2[...] + b2[...]).astype(BF)[None]
    second_all.send()

    up_move.ready()
    dn_move.ready()

    def feed(k, carry):
        @pl.when(k == 1)
        def _():
            second_all.near()
            dy_all.near()

        @pl.when(k == 2)
        def _():
            second_all.take()

        @pl.when(k == 3)
        def _():
            second_all.last()
            dy_all.last()

        s = pl.ds(p.rank_of(k), 1)
        value, slope = gelu_parts(mm(second[s][0], up[...]) + ub[...])
        value = value.astype(BF)
        hidden[s] = value[None]
        back = (mm_nt(dy[s][0], dn[...]) * slope).astype(BF)
        dpre[s] = back[None]
        s_part[s] = mm_nt(back, up[...]).astype(BF)[None]

        @pl.when(k == 1)
        def _():
            s_sum.give_near()

        @pl.when(k == 3)
        def _():
            s_sum.give_far()

        o_part[s] = mm(value, dn[...]).astype(BF)[None]
        return carry

    lax.fori_loop(0, 4, feed, 0)
    s_sum.ship()
    o_sum.give_far()
    o_sum.give_near()
    units = hidden.shape[2]
    for c in range(4):
        cols = slice(c * units // 4, (c + 1) * units // 4)
        dg[cols, :] = mm_tn(hidden[:, :, cols].reshape(length, units // 4), dy[...].reshape(length, width)).astype(BF)
    dn_grad.scatter()
    for c in range(4):
        cols = slice(c * width // 4, (c + 1) * width // 4)
        ug[cols, :] = mm_tn(second[:, :, cols].reshape(length, width // 4), dpre[...].reshape(length, units)).astype(BF)
    up_grad.scatter()

    grad = dy[pl.ds(rank, 1)][0].astype(F32)
    total = s_sum.total()
    normed, scale = norm(middle[...])
    dmiddle[...] = grad + norm_back(total, normed, scale, g2[...])
    low = dmiddle[...].astype(BF)
    dmid[pl.ds(rank, 1)] = low[None]
    dmid_all.send()
    o_sum.ship()
    sm[...] = jnp.zeros(sm.shape, F32)
    sm[0:1, :] = jnp.sum(total * normed, 0, keepdims=True)
    sm[1:2, :] = jnp.sum(total, 0, keepdims=True)
    sm[2:3, :] = jnp.sum(low.astype(F32), 0, keepdims=True)
    sm[3:4, :] = jnp.sum(grad, 0, keepdims=True)
    bias_sum = jnp.sum(dpre[...].reshape(length, units).astype(F32), 0, keepdims=True)
    for q in range(4):
        sm[8 + q : 9 + q, :] = jnp.where(rank == q, bias_sum, 0.0)
    for t in range(3):
        acc[t] = jnp.zeros((length, share), F32)
    dmid_all.take()

    ctx_cols = slice(3 * share, 4 * share)

    def to_context(k):
        s = pl.ds(p.rank_of(k), 1)
        value = mm_nt(dmid[s][0], ow[...]).astype(BF)
        hidden[s, :, ctx_cols] = value[None]
        for h in range(heads):
            cols = slice(h * HD, (h + 1) * HD)
            product = value[:, cols].astype(F32) * own[s, :, cols][0].astype(F32)
            stats[h, strip(p.rank_of(k)), 1:2] = jnp.sum(product, -1, keepdims=True)

    to_context(0)
    dmid_all.near()
    to_context(1)
    to_context(2)
    dmid_all.last()
    to_context(3)
    og[...] = mm_tn(own[...].reshape(length, share), dmid[...].reshape(length, width)).astype(BF)
    ow_grad.scatter()
    a_sum.finish()

    mirror = 1 - p.odd
    for g in range(4):

        def block(e, carry):
            i = (g + e) + mirror * (3 - g - (g + e))
            j = g + mirror * (3 - (g + e) - g)
            qs, ks = strip(i), strip(j)
            place_q = i * rows + lax.broadcasted_iota(jnp.int32, (rows, rows), 0)
            place_k = j * rows + lax.broadcasted_iota(jnp.int32, (rows, rows), 1)
            allowed = (segc[qs, 0:1] == seg[0:1, ks]) & (place_q >= place_k)
            for h in range(heads):
                cols = slice(h * HD, (h + 1) * HD)
                q = mixed[qs, cols]
                k = mixed[ks, share + h * HD : share + (h + 1) * HD]
                v = mixed[ks, 2 * share + h * HD : 2 * share + (h + 1) * HD]
                head = hidden[pl.ds(i, 1), :, 3 * share + h * HD : 3 * share + (h + 1) * HD][0]
                scores = jnp.where(allowed, mm_nt(q, k) * factor, -1e30)
                probs = jnp.exp(scores - stats[h, qs, 0:1])
                acc[2, ks, cols] += mm_tn(probs.astype(BF), head)
                back = (probs * (mm_nt(head, v) - stats[h, qs, 1:2])).astype(BF)
                acc[0, qs, cols] += mm(back, k)
                acc[1, ks, cols] += mm_tn(back, q)
            return carry

        lax.fori_loop(0, 4 - g, block, 0)
        r = g + mirror * (3 - 2 * g)
        total = None
        for t in range(3):
            value = acc[t, strip(r), :]
            low = (value * factor if t < 2 else value).astype(BF)
            hidden[pl.ds(r, 1), :, t * share : (t + 1) * share] = low[None]
            term = mm_nt(low, wq[t])
            total = term if total is None else total + term
        a_part[pl.ds(r, 1)] = total.astype(BF)[None]
        if g % 2 == 0:
            pl.when(r == p.rank_of(3))(f_sum.give_far)
            pl.when(r == p.rank_of(2))(f_sum.ship)
        else:
            pl.when(r == p.rank_of(1))(f_sum.give_near)

    for t in range(3):
        cols = slice(t * share, (t + 1) * share)
        low = hidden[:, :, cols].reshape(length, share)
        pg[t] = mm_tn(first[...].reshape(length, width), low).astype(BF)
        bias = jnp.sum(low.astype(F32), 0, keepdims=True)
        line = (6, 7, 12)[t]
        for q in range(4):
            sm[line : line + 1, q * share : (q + 1) * share] = jnp.where(rank == q, bias, 0.0)
    pj_grad.scatter()
    dn_grad.combine()
    up_grad.combine()

    total = f_sum.total()
    normed, scale = norm(xs[...].astype(F32))
    rows_out[0] = (dmiddle[...] + norm_back(total, normed, scale, g1[...])).astype(BF)

    @p.at_home
    def _():
        tg_home().start()

    @p.if_swapped
    def _():
        tg_back().start()

    sm[4:5, :] = jnp.sum(total * normed, 0, keepdims=True)
    sm[5:6, :] = jnp.sum(total, 0, keepdims=True)

    def sm_copy(k, t):
        return remote(sm, sm_in.at[k], ss_sm.at[k], rs_sm.at[k], p.along(t))

    for k, t in enumerate(others):
        sm_copy(k, t).start()
    rows_out[1] = (middle[...] + (o_sum.total() + dwb[...])).astype(BF)

    @p.at_home
    def _():
        out_home().start()

    @p.if_swapped
    def _():
        out_back().start()

    ow_grad.combine()
    p.at_home(dn_grad.final)
    p.at_home(up_grad.final)
    pj_grad.combine()
    p.at_home(ow_grad.final)
    sm_sum = sm[...]
    for k, t in enumerate(others):
        sm_copy(k, t).wait_recv()
        sm_sum = sm_sum + sm_in[k]
    smp[pl.ds(p.d, 1)] = sm_sum[None]
    sm_all = Plane(p, smp, ss_sp, rs_sp)
    sm_all.send()
    p.at_home(dn_grad.relay)
    p.at_home(pj_grad.final)
    sm_all.take()
    p.at_home(up_grad.relay)
    sm_all.rest()
    small_out[...] = jnp.sum(smp[...], 0)
    p.at_home(ow_grad.relay)
    p.at_home(pj_grad.relay)

    for group in (first_all, second_all, dy_all, dmid_all, s_sum, o_sum, f_sum, sm_all):
        group.finish()
    for k, t in enumerate(others):
        sm_copy(k, t).wait_send()

    @p.at_home
    def _():
        seg_give().wait_send()
        tg_home().wait()
        out_home().wait()

    @p.if_swapped
    def _():
        for copy in (x_swap(), bq_swap(), ub_swap(), cot_swap(rank), tg_back(), out_back()):
            copy.wait_send()
        tg_back().wait_recv()
        out_back().wait_recv()
        for move in (wq_move, ow_move, up_move, dn_move):
            move.finish()

    for grad_sum in (dn_grad, up_grad, pj_grad, ow_grad):
        grad_sum.finish()


def run_layer(
    x, cot, seg_ids, g1, b1, wq, bq, ow, ob, g2, b2, upw, upb, dnw, dnb,
):
    rows, width = x.shape
    share = wq.shape[2]
    length = 4 * rows
    heads = share // HD
    units = upw.shape[1]
    vm = pl.BlockSpec(memory_space=VMEM)
    hbm = pl.BlockSpec(memory_space=pl.ANY)
    token = (rows, width)
    outs = [
        (hbm, token, BF), (hbm, token, BF), (vm, (16, width), F32), (hbm, (3, width, share), BF),
        (hbm, (share, width), BF), (hbm, (width, units), BF), (hbm, (units, width), BF),
    ]
    four = VMEM((4,) + token, BF)
    sums = [VMEM((2,) + token, BF), VMEM(token, BF), VMEM(token, BF)]
    quarters = [(units // 4, width), (width // 4, units), (3, width // 4, share), (share // 4, width)]
    pair = lambda n: [DMA((n,)), DMA((n,))]
    return pl.pallas_call(
        layer,
        out_shape=[jax.ShapeDtypeStruct(s, t) for _, s, t in outs],
        in_specs=[hbm, hbm, vm, vm, vm, hbm, vm, hbm, vm, vm, vm, hbm, vm, hbm, vm],
        out_specs=[m for m, _, _ in outs],
        scratch_shapes=[
            VMEM(token, BF), VMEM((8, length), jnp.int32), VMEM((length, HD), jnp.int32), four, four, four, four,
            VMEM((length, 3 * share), BF), VMEM((4, rows, share), BF), VMEM((heads, length, HD), F32),
            VMEM((3, width, share), BF), VMEM((3, share), F32), VMEM((share, width), BF), VMEM((width, units), BF),
            VMEM((1, units), F32), VMEM((units, width), BF),
            four, *sums, four, *sums, four, *sums, *sums,
            VMEM((4, rows, units), BF), VMEM((4, rows, units), BF),
            VMEM((units, width), BF), VMEM((width, units), BF), VMEM((3, width, share), BF), VMEM((share, width), BF),
            *[VMEM((3,) + q, BF) for q in quarters], *[VMEM(q, BF) for q in quarters], *[VMEM(q, BF) for q in quarters],
            VMEM((3, length, share), F32), VMEM(token, F32), VMEM(token, F32), VMEM((2,) + token, BF),
            VMEM((16, width), F32), VMEM((3, 16, width), F32), VMEM((8, 16, width), F32),
            *pair(7), *pair(3), *pair(3), *pair(3), *pair(3), *pair(3), *pair(3), *pair(3), *pair(3),
            *pair(4), *pair(4), *pair(4), *pair(4), *pair(12), *pair(12), *pair(12), *pair(12), *pair(3), *pair(7),
        ],
        compiler_params=pltpu.CompilerParams(collective_id=0, has_side_effects=True, vmem_limit_bytes=64 << 20),
        name="layer",
    )(
        x, cot, jnp.broadcast_to(seg_ids.reshape(1, length), (8, length)), g1.reshape(1, width), b1.reshape(1, width),
        wq, bq, ow, ob.reshape(1, width), g2.reshape(1, width), b2.reshape(1, width), upw, upb.reshape(1, units),
        dnw, dnb.reshape(1, width),
    )


def shards(
    tokens, seg_ids, cotangent, first_gain, first_shift, project_weight, project_bias, out_weight, out_bias,
    second_gain, second_shift, up_weight, up_bias, down_weight, down_bias,
):
    share = project_weight.shape[2]
    output, tokens_grad, sums, *grads = run_layer(
        tokens, cotangent, seg_ids, first_gain, first_shift, project_weight, project_bias, out_weight, out_bias,
        second_gain, second_shift, up_weight, up_bias, down_weight, down_bias,
    )
    reduced = (sums, *[g.astype(jnp.float32) for g in grads])
    if lax.axis_size("dp") > 8:
        reduced = jax.tree.map(lambda v: v * 0.125, lax.psum(reduced, "dp"))
    sums, project_grad, outw_grad, up_grad, down_grad = reduced
    z = lax.axis_index("mp")
    upbias_grad = lax.dynamic_index_in_dim(sums, 8 + z, 0, False)
    pbias_grad = lax.dynamic_slice_in_dim(jnp.stack([sums[6], sums[7], sums[12]]), z * share, share, 1)
    return (
        output, tokens_grad, sums[4], sums[5], project_grad, pbias_grad, outw_grad, sums[2], sums[0], sums[1],
        up_grad, upbias_grad, down_grad, sums[3],
    )


def solution(mesh):
    in_specs = (
        P(("dp", "mp"), None),
        P("dp"),
        P(("dp", "mp"), None),
        P(),
        P(),
        P(None, None, "mp"),
        P(None, "mp"),
        P("mp", None),
        P(),
        P(),
        P(),
        P(None, "mp"),
        P("mp"),
        P("mp", None),
        P(),
    )
    out_specs = (
        P(("dp", "mp"), None),
        P(("dp", "mp"), None),
        P(),
        P(),
        P(None, None, "mp"),
        P(None, "mp"),
        P("mp", None),
        P(),
        P(),
        P(),
        P(None, "mp"),
        P("mp"),
        P("mp", None),
        P(),
    )
    return jax.shard_map(shards, mesh=mesh, in_specs=in_specs, out_specs=out_specs, check_vma=False)
```

```python
import math

import jax
import jax.numpy as jnp
from jax import lax
from jax.experimental import pallas as pl
from jax.experimental.pallas import tpu as pltpu
from jax.sharding import PartitionSpec as P

HD = 128
EPS = 1e-05
BF = jnp.bfloat16
F32 = jnp.float32
MESH = pl.DeviceIdType.MESH
VMEM = pltpu.VMEM
DMA = pltpu.SemaphoreType.DMA
GELU_A = 0.7978845608
GELU_B = 0.044715


def mm(left, right):
    return jnp.dot(left, right, preferred_element_type=F32)


def mm_nt(left, right):
    return lax.dot_general(left, right, (((1,), (1,)), ((), ())), preferred_element_type=F32)


def mm_tn(left, right):
    return lax.dot_general(left, right, (((0,), (0,)), ((), ())), preferred_element_type=F32)


def remote(src, dst, ss, rs, device):
    return pltpu.make_async_remote_copy(
        src_ref=src, dst_ref=dst, send_sem=ss, recv_sem=rs, device_id=device, device_id_type=MESH
    )


def local(src, dst, sem):
    return pltpu.make_async_copy(src, dst, sem)


def barrier(devices):
    sem = pltpu.get_barrier_semaphore()
    for device in devices:
        pl.semaphore_signal(sem, 1, device_id=device, device_id_type=MESH)
    return lambda: pl.semaphore_wait(sem, len(devices))


def start(copy):
    copy.start()


def wait(copy):
    copy.wait()


def sent(copy):
    copy.wait_send()


def came(copy):
    copy.wait_recv()


def norm(values):
    mean = jnp.mean(values, -1, keepdims=True)
    centered = values - mean
    var = jnp.mean(centered * centered, -1, keepdims=True)
    scale = lax.rsqrt(var + EPS)
    return centered * scale, scale


def norm_back(grad, normed, scale, gain):
    scaled = grad * gain
    return scale * (
        scaled - jnp.mean(scaled, -1, keepdims=True) - normed * jnp.mean(scaled * normed, -1, keepdims=True)
    )


def gelu_parts(v):
    square = v * v
    t = jnp.tanh(GELU_A * v * (1.0 + GELU_B * square))
    half = 0.5 * (1.0 + t)
    slope = half + 0.5 * v * (1.0 - t * t) * (GELU_A * (1.0 + 3.0 * GELU_B * square))
    return v * half, slope


class Place:
    def __init__(self):
        self.z = lax.axis_index("mp")
        self.dp = lax.axis_index("dp")
        self.d = lax.rem(self.dp, 8)
        self.base = self.dp - self.d
        self.core = lax.rem(self.d, 2)
        self.column = self.d // 2
        bit_x = lax.rem(self.column, 2)
        bit_y = self.column // 2
        self.step_x = 1 - 2 * bit_x
        self.step_y = 2 - 4 * bit_y
        self.sibling = self.dp + 1 - 2 * self.core
        self.swapped = lax.rem(self.core + self.z // 2, 2)
        self.far = lax.rem(self.z + 2, 4)
        self.rank = lax.rem(self.z + 2 * self.swapped, 4)
        self.odd = lax.rem(self.z, 2)

    def column_at(self, i):
        return self.column + (i % 2) * self.step_x + (i // 2) * self.step_y

    def chip(self, i):
        return {"dp": self.base + 2 * self.column_at(i) + self.core, "mp": self.z}

    def along(self, z):
        return {"dp": self.dp, "mp": z}

    def to_sibling(self):
        return {"dp": self.sibling, "mp": self.z}

    def across(self):
        return {"dp": self.dp, "mp": self.z + 1 - 2 * self.odd}

    def partner(self):
        return {"dp": self.sibling, "mp": self.far}

    def rank_of(self, k):
        return lax.rem(self.rank + (k // 2) * (1 - 2 * self.odd) + 2 * (k % 2), 4)

    def at_home(self, body):
        pl.when(self.swapped == 0)(body)

    def if_swapped(self, body):
        pl.when(self.swapped == 1)(body)


class Gather:
    def __init__(self, p, buf, ss, rs):
        self.p, self.buf, self.ss, self.rs = p, buf, ss, rs
        self.half = buf.shape[1] // 2

    def _copy(self, k, i, c, device):
        view = self.buf.at[self.p.rank_of(k), pl.ds(c * self.half, self.half)]
        return remote(view, view, self.ss.at[i, c], self.rs.at[i, c], device)

    def send(self, c):
        self._copy(0, 0, c, self.p.across()).start()
        self._copy(0, 1, c, self.p.to_sibling()).start()

    def take(self, c):
        self._copy(2, 0, c, self.p.across()).wait_recv()
        self._copy(2, 2, c, self.p.to_sibling()).start()

    def near(self, c):
        self._copy(1, 1, c, self.p.to_sibling()).wait_recv()

    def last(self, c):
        self._copy(3, 2, c, self.p.to_sibling()).wait_recv()

    def both(self, step):
        step(0)
        step(1)

    def finish(self):
        for c in range(2):
            self._copy(0, 0, c, self.p.across()).wait_send()
            self._copy(0, 1, c, self.p.to_sibling()).wait_send()
            self._copy(2, 2, c, self.p.to_sibling()).wait_send()


class Sum:
    def __init__(self, p, parts, got, out, into, ss, rs):
        self.p, self.parts, self.got, self.out, self.into, self.ss, self.rs = p, parts, got, out, into, ss, rs
        self.half = parts.shape[1] // 2

    def _cut(self, c):
        return pl.ds(c * self.half, self.half)

    def _give(self, n, c):
        src = self.parts.at[self.p.rank_of(1 + 2 * n), self._cut(c)]
        return remote(src, self.got.at[n, self._cut(c)], self.ss.at[n, c], self.rs.at[n, c], self.p.to_sibling())

    def _ship(self, c):
        cut = self._cut(c)
        return remote(self.out.at[cut], self.into.at[cut], self.ss.at[2, c], self.rs.at[2, c], self.p.across())

    def _part(self, k, c):
        return self.parts[pl.ds(self.p.rank_of(k), 1), self._cut(c)][0].astype(F32)

    def give_far(self, c):
        self._give(1, c).start()

    def give_near(self, c):
        self._give(0, c).start()

    def ship(self, c):
        self._give(1, c).wait_recv()
        self.out[self._cut(c), :] = (self._part(2, c) + self.got[1, self._cut(c)].astype(F32)).astype(BF)
        self._ship(c).start()

    def done(self, r):
        for k, step in ((3, self.give_far), (2, self.ship), (1, self.give_near)):

            @pl.when(r == self.p.rank_of(k))
            def _():
                step(0)
                step(1)

    def total(self, c):
        self._give(0, c).wait_recv()
        total = self._part(0, c) + self.got[0, self._cut(c)].astype(F32)
        self._ship(c).wait_recv()
        return total + self.into[self._cut(c), :].astype(F32)

    def finish(self):
        for c in range(2):
            self._give(0, c).wait_send()
            self._give(1, c).wait_send()
            self._ship(c).wait_send()


class Weight:
    def __init__(self, p, src, buf, ss, rs, pieces):
        self.p, self.src, self.buf, self.ss, self.rs, self.pieces = p, src, buf, ss, rs, pieces
        self.size = buf.shape[0] // (4 * pieces)

    def _cut(self, ref, column, n):
        return ref.at[pl.ds(pl.multiple_of((column * self.pieces + n) * self.size, self.size), self.size)]

    def _own(self):
        return local(self.src, self.buf, self.ss.at[0, 0])

    def _swap(self, n):
        src, dst = self._cut(self.src, self.p.column, n), self._cut(self.buf, self.p.column, n)
        return remote(src, dst, self.ss.at[0, n], self.rs.at[0, n], self.p.partner())

    def _share(self, i, column, n):
        view = self._cut(self.buf, column, n)
        return remote(view, view, self.ss.at[i, n], self.rs.at[i, n], self.p.chip(i))

    def home(self):
        self._own().start()

    def swap(self, n=0):
        self._swap(n).start()

    def take(self, n=0):
        self._swap(n).wait_recv()
        for i in (1, 2, 3):
            self._share(i, self.p.column, n).start()

    def ready(self):
        self.p.at_home(lambda: self._own().wait())

        @self.p.if_swapped
        def _():
            for n in range(self.pieces):
                for i in (1, 2, 3):
                    self._share(i, self.p.column_at(i), n).wait_recv()

    def finish(self):
        for n in range(self.pieces):
            self._swap(n).wait_send()
            for i in (1, 2, 3):
                self._share(i, self.p.column, n).wait_send()


class Grad:
    def __init__(self, p, buf, into, last, total, far, out, ss, rs):
        self.p, self.buf, self.into, self.last, self.sum, self.far, self.out = p, buf, into, last, total, far, out
        self.ss, self.rs = ss, rs
        self.size = buf.shape[0] // 8

    def _at(self, ref, column, n):
        return ref.at[pl.ds(pl.multiple_of((2 * column + n) * self.size, self.size), self.size)]

    def _own(self, n):
        return self.sum.at[pl.ds(n * self.size, self.size)]

    def _step(self, n, m):
        return m if n == 0 or m == 3 else 3 - m

    def _column(self, n, m):
        return self.p.column_at(self._step(n, m)) if m else self.p.column

    def _chip(self, n, m):
        return self.p.chip(self._step(n, m))

    def _copy(self, src, dst, i, n, device):
        return remote(src, dst, self.ss.at[i, n], self.rs.at[i, n], device)

    def _first(self, n, k):
        src = self._at(self.buf, self._column(n, (1, 3)[k]), n)
        return self._copy(src, self.into.at[n, k], k, n, self._chip(n, 1))

    def _second(self, n):
        return self._copy(self.into.at[n, 1], self.last.at[n], 2, n, self._chip(n, 2))

    def _home(self):
        return self._copy(self.sum, self.far, 3, 0, self.p.along(self.p.far))

    def _keep(self):
        return local(self.sum, self.out.at[pl.ds(pl.multiple_of(2 * self.p.column * self.size, 2 * self.size), 2 * self.size)], self.ss.at[3, 1])

    def _spread(self, n, m):
        return self._copy(self._own(n), self._at(self.out, self.p.column, n), 3 + m, n, self._chip(n, m))

    def _arrived(self, n, m):
        return self._copy(self._own(n), self._at(self.out, self._column(n, m), n), 3 + m, n, self._chip(n, m))

    def _pass(self, n):
        view = self._at(self.out, self._column(n, 2), n)
        return self._copy(view, view, 6, n, self._chip(n, 1))

    def _passed(self, n):
        view = self._at(self.out, self._column(n, 3), n)
        return self._copy(view, view, 6, n, self._chip(n, 1))

    def _hand(self, n, m):
        view = self._at(self.out, self._column(n, m), n)
        return self._copy(view if m else self._own(n), view, 7 + m, n, self.p.to_sibling())

    def scatter(self):
        for n in range(2):
            self._first(n, 1).start()
            self._first(n, 0).start()

    def middle(self):
        for n in range(2):
            self._first(n, 1).wait_recv()
            value = self._at(self.buf, self._column(n, 2), n)[...].astype(F32) + self.into[n, 1].astype(F32)
            self.into[n, 1] = value.astype(BF)
            self._second(n).start()

    def combine(self):
        for n in range(2):
            self._first(n, 0).wait_recv()
            self._second(n).wait_recv()
            total = self._at(self.buf, self.p.column, n)[...].astype(F32) + self.into[n, 0].astype(F32)
            self._own(n)[...] = (total + self.last[n].astype(F32)).astype(BF)
        self.p.if_swapped(lambda: self._home().start())

    def final(self):
        self._home().wait_recv()
        self.sum[...] = (self.sum[...].astype(F32) + self.far[...].astype(F32)).astype(BF)
        for n in range(2):
            self._spread(n, 2).start()
            self._spread(n, 1).start()
        for n in range(2):
            self._hand(n, 0).start()
        self._keep().start()

    def relay(self):
        for n in range(2):
            self._arrived(n, 2).wait_recv()
            self._pass(n).start()
            self._hand(n, 2).start()

    def relay_last(self):
        for n in range(2):
            self._arrived(n, 1).wait_recv()
            self._hand(n, 1).start()
            self._passed(n).wait_recv()
            self._hand(n, 3).start()

    def finish(self):
        for n in range(2):
            self._first(n, 0).wait_send()
            self._first(n, 1).wait_send()
            self._second(n).wait_send()

        @self.p.at_home
        def _():
            for n in range(2):
                for m in (1, 2):
                    self._spread(n, m).wait_send()
                self._pass(n).wait_send()
                for m in range(4):
                    self._hand(n, m).wait_send()
            self._keep().wait()

        @self.p.if_swapped
        def _():
            self._home().wait_send()
            for n in range(2):
                for m in range(4):
                    self._hand(n, m).wait_recv()


class Plane:
    def __init__(self, p, buf, ss, rs):
        self.p, self.buf, self.ss, self.rs = p, buf, ss, rs

    def _copy(self, column, core, i, device):
        view = self.buf.at[2 * column + core]
        return remote(view, view, self.ss.at[i], self.rs.at[i], device)

    def send(self):
        p = self.p
        for i in (1, 2, 3):
            self._copy(p.column, p.core, i, p.chip(i)).start()
        self._copy(p.column, p.core, 0, p.to_sibling()).start()

    def take(self):
        p = self.p
        for i in (1, 2, 3):
            self._copy(p.column_at(i), p.core, i, p.chip(i)).wait_recv()
            self._copy(p.column_at(i), p.core, 3 + i, p.to_sibling()).start()

    def rest(self):
        p = self.p
        self._copy(p.column, 1 - p.core, 0, p.to_sibling()).wait_recv()
        for i in (1, 2, 3):
            self._copy(p.column_at(i), 1 - p.core, 3 + i, p.to_sibling()).wait_recv()

    def finish(self):
        p = self.p
        self._copy(p.column, p.core, 0, p.to_sibling()).wait_send()
        for i in (1, 2, 3):
            self._copy(p.column, p.core, i, p.chip(i)).wait_send()
            self._copy(p.column_at(i), p.core, 3 + i, p.to_sibling()).wait_send()


def layer(
    x_ref, cot, seg_ref, g1_ref, b1_ref, wq_ref, bq_ref, ow_ref, ob_ref, g2_ref, b2_ref, up_ref, ub_ref, dn_ref, db_ref,
    output, tokens_grad, small_out, pg_out, og_out, ug_out, dg_out,
    xs, seg, segc, first, second, dy, dmid, mixed, own, probs, delta, wq, bq, ow, up, ub, dn,
    a_part, a_got, a_out, a_in, s_part, s_got, s_out, s_in, o_part, o_got, o_out, o_in,
    hidden, dpre, dg, ug, pg, og, dg_in, ug_in, pg_in, og_in, dg_last, ug_last, pg_last, og_last, dg_sum, ug_sum, pg_sum, og_sum,
    dg_far, ug_far, pg_far, og_far, g1, b1, ob, g2, b2, dwb, acc, middle, dmiddle, rows_out, sm, sm_in, smp,
    ss_vec, ss_in, rs_in, ss_first, rs_first, ss_second, rs_second, ss_dy, rs_dy, ss_dmid, rs_dmid,
    ss_a, rs_a, ss_s, rs_s, ss_o, rs_o, ss_f, rs_f, ss_wq, rs_wq, ss_ow, rs_ow, ss_up, rs_up, ss_dn, rs_dn,
    ss_dg, rs_dg, ss_ug, rs_ug, ss_pg, rs_pg, ss_og, rs_og, ss_sm, rs_sm, ss_sp, rs_sp,
):
    p = Place()
    rows, width = xs.shape
    half = rows // 2
    share = wq.shape[2]
    heads = share // HD
    factor = 1.0 / math.sqrt(HD)
    length = 4 * rows
    others = [lax.rem(p.z + k, 4) for k in (1, 2, 3)]
    enter = barrier([p.to_sibling(), p.partner()] + [p.along(t) for t in others] + [p.chip(i) for i in (1, 2, 3)])
    rank = p.rank
    halves = [slice(0, half), slice(half, rows)]

    def strip(index):
        return pl.ds(pl.multiple_of(index * rows, rows), rows)

    wq_moves = [Weight(p, wq_ref.at[t], wq.at[t], ss_wq.at[t], rs_wq.at[t], 1) for t in range(3)]
    ow_move = Weight(p, ow_ref, ow, ss_ow, rs_ow, 1)
    up_move = Weight(p, up_ref, up, ss_up, rs_up, 2)
    dn_move = Weight(p, dn_ref, dn, ss_dn, rs_dn, 2)
    moves = (*wq_moves, ow_move, up_move, dn_move)
    first_all = Gather(p, first, ss_first, rs_first)
    second_all = Gather(p, second, ss_second, rs_second)
    dy_all = Gather(p, dy, ss_dy, rs_dy)
    dmid_all = Gather(p, dmid, ss_dmid, rs_dmid)
    a_sum = Sum(p, a_part, a_got, a_out, a_in, ss_a, rs_a)
    s_sum = Sum(p, s_part, s_got, s_out, s_in, ss_s, rs_s)
    o_sum = Sum(p, o_part, o_got, o_out, o_in, ss_o, rs_o)
    f_sum = Sum(p, a_part, a_got, a_out, a_in, ss_f, rs_f)
    dn_grad = Grad(p, dg, dg_in, dg_last, dg_sum, dg_far, dg_out, ss_dg, rs_dg)
    up_grad = Grad(p, ug, ug_in, ug_last, ug_sum, ug_far, ug_out, ss_ug, rs_ug)
    ow_grad = Grad(p, og, og_in, og_last, og_sum, og_far, og_out, ss_og, rs_og)
    pj_grads = [
        Grad(
            p, pg.at[t], pg_in.at[t], pg_last.at[t], pg_sum.at[t], pg_far.at[t], pg_out.at[t], ss_pg.at[t], rs_pg.at[t]
        )
        for t in range(3)
    ]

    def x_home():
        return local(x_ref, xs, ss_in.at[0])

    def cot_home():
        return local(cot, dy.at[rank], ss_in.at[1])

    def x_swap(c):
        cut = pl.ds(c * half, half)
        return remote(x_ref.at[cut], xs.at[cut], ss_in.at[7 + c], rs_in.at[7 + c], p.partner())

    def cot_swap(slot):
        return remote(cot, dy.at[slot], ss_in.at[1], rs_in.at[1], p.partner())

    def bq_swap():
        return remote(bq_ref, bq, ss_in.at[2], rs_in.at[2], p.partner())

    def ub_swap():
        return remote(ub_ref, ub, ss_in.at[3], rs_in.at[3], p.partner())

    def seg_give():
        return remote(seg_ref, seg, ss_in.at[4], rs_in.at[4], p.to_sibling())

    def back_swap(n, out, c):
        cut = pl.ds(c * half, half)
        i = 9 + 2 * n + c
        return remote(rows_out.at[n, cut], out.at[cut], ss_in.at[i], rs_in.at[i], p.partner())

    def back_home(n, out, c):
        cut = pl.ds(c * half, half)
        return local(rows_out.at[n, cut], out.at[cut], ss_in.at[9 + 2 * n + c])

    def put_back(n, out, c):
        p.at_home(lambda: back_home(n, out, c).start())
        p.if_swapped(lambda: back_swap(n, out, c).start())

    vectors = [
        local(a, b, ss_vec.at[i])
        for i, (a, b) in enumerate(
            ((g1_ref, g1), (b1_ref, b1), (ob_ref, ob), (g2_ref, g2), (b2_ref, b2), (db_ref, dwb))
        )
    ]
    kept = [local(a, b, ss_vec.at[6 + i]) for i, (a, b) in enumerate(((bq_ref, bq), (ub_ref, ub), (seg_ref, seg)))]

    @p.at_home
    def _():
        x_home().start()

    for copy in vectors:
        copy.start()

    @p.at_home
    def _():
        for copy in kept:
            copy.start()
        for move in moves:
            move.home()
        cot_home().start()

    enter()

    @p.if_swapped
    def _():
        x_swap(0).start()
        x_swap(1).start()

    @p.at_home
    def _():
        seg_give().start()
        x_home().wait()
        for copy in kept:
            copy.wait()

    for copy in vectors:
        copy.wait()
    for c in range(2):

        @p.if_swapped
        def _():
            x_swap(c).wait_recv()
            wq_moves[c].swap()

        normed, _ = norm(xs[halves[c], :].astype(F32))
        first[pl.ds(rank, 1), halves[c]] = (normed * g1[...] + b1[...]).astype(BF)[None]
        first_all.send(c)

    @p.if_swapped
    def _():
        bq_swap().start()
        wq_moves[2].swap()
        wq_moves[0].take()
        ow_move.swap()
        wq_moves[1].take()
        ub_swap().start()
        up_move.swap(0)
        wq_moves[2].take()
        up_move.swap(1)
        seg_give().wait_recv()
        bq_swap().wait_recv()

    segc[...] = jnp.transpose(jnp.broadcast_to(seg[0:1, :], (HD, length)))

    def project(k):
        s = p.rank_of(k)
        block = first[pl.ds(s, 1)][0]
        for t in range(3):
            value = mm(block, wq[t]) + bq[t : t + 1, :]
            mixed[strip(s), t * share : (t + 1) * share] = value.astype(BF)

    @p.at_home
    def _():
        for move in wq_moves:
            move.ready()
        project(0)

    first_all.both(first_all.take)

    @p.at_home
    def _():
        project(2)

    @p.if_swapped
    def _():
        for move in wq_moves:
            move.ready()
        project(0)
        project(2)
        ow_move.take()

    first_all.both(first_all.near)
    project(1)
    first_all.both(first_all.last)
    project(3)

    @p.if_swapped
    def _():
        up_move.take(0)
        dn_move.swap(0)
        dn_move.swap(1)
        ub_swap().wait_recv()

    @p.at_home
    def _():
        cot_home().wait()
        dy_all.both(dy_all.send)

    ow_move.ready()
    for r in reversed(range(4)):
        span = (r + 1) * rows
        top = r * rows
        place_q = top + lax.broadcasted_iota(jnp.int32, (rows, span), 0)
        place_k = lax.broadcasted_iota(jnp.int32, (rows, span), 1)
        allowed = (segc[top : top + rows, 0:1] == seg[0:1, 0:span]) & (place_q >= place_k)
        for h in range(heads):
            q = mixed[top : top + rows, h * HD : (h + 1) * HD]
            k = mixed[0:span, share + h * HD : share + (h + 1) * HD]
            v = mixed[0:span, 2 * share + h * HD : 2 * share + (h + 1) * HD]
            scores = jnp.where(allowed, mm_nt(q, k) * factor, -1e30)
            expo = jnp.exp(scores - jnp.max(scores, -1, keepdims=True))
            low = (expo / jnp.sum(expo, -1, keepdims=True)).astype(BF)
            for j in range(r + 1):
                probs[h, r * (r + 1) // 2 + j] = low[:, j * rows : (j + 1) * rows]
            own[r, :, h * HD : (h + 1) * HD] = mm(low, v).astype(BF)
        a_part[r] = mm(own[r], ow[...]).astype(BF)
        a_sum.done(r)

    @p.if_swapped
    def _():
        cot_swap(p.z).start()
        up_move.take(1)

    for c in range(2):
        cut = halves[c]
        middle[cut, :] = xs[cut, :].astype(F32) + (a_sum.total(c) + ob[...])
        normed, _ = norm(middle[cut, :])
        second[pl.ds(rank, 1), cut] = (normed * g2[...] + b2[...]).astype(BF)[None]
        second_all.send(c)

    @p.if_swapped
    def _():
        dn_move.take(0)
        dn_move.take(1)


    up_move.ready()

    class Rows:
        def __init__(self, k):
            late = k // 2
            self.top = p.rank_of(k - late * (k - 2))
            self.low = p.rank_of(k + late * (3 - k))
            self.at_top = pl.ds(pl.multiple_of(late * (k - 2) * half, half), half)
            self.at_low = pl.ds(pl.multiple_of(half - late * (3 - k) * half, half), half)

        def load(self, ref):
            return jnp.concatenate([ref[pl.ds(self.top, 1), self.at_top][0], ref[pl.ds(self.low, 1), self.at_low][0]], 0)

        def store(self, ref, value):
            ref[pl.ds(self.top, 1), self.at_top] = value[None, :half]
            ref[pl.ds(self.low, 1), self.at_low] = value[None, half:]

    def feed(k, carry):
        @pl.when(k == 1)
        def _():
            second_all.both(second_all.near)

        @pl.when(k == 2)
        def _():
            @p.if_swapped
            def _():
                cot_swap(rank).wait_recv()
                dy_all.both(dy_all.send)

            second_all.take(0)
            second_all.last(0)

        @pl.when(k == 3)
        def _():
            second_all.take(1)
            second_all.last(1)

        at = Rows(k)
        value, slope = gelu_parts(mm(at.load(second), up[...]) + ub[...])
        at.store(hidden, value.astype(BF))
        at.store(dpre, slope.astype(BF))
        return carry

    lax.fori_loop(0, 4, feed, 0)

    dn_move.ready()
    dy_all.both(dy_all.take)
    dy_all.both(dy_all.near)
    dy_all.both(dy_all.last)

    def feed_back(n, carry):
        k = 2 + n - 4 * (n // 2)
        at = Rows(k)
        back = (mm_nt(at.load(dy), dn[...]) * at.load(dpre).astype(F32)).astype(BF)
        at.store(dpre, back)
        at.store(s_part, mm_nt(back, up[...]).astype(BF))

        @pl.when(k == 2)
        def _():
            s_sum.give_far(0)

        @pl.when(k == 3)
        def _():
            s_sum.give_far(1)
            s_sum.ship(0)

        @pl.when(k == 0)
        def _():
            s_sum.ship(1)

        @pl.when(k == 1)
        def _():
            s_sum.give_near(0)
            s_sum.give_near(1)

        at.store(o_part, mm(at.load(hidden), dn[...]).astype(BF))
        return carry

    lax.fori_loop(0, 4, feed_back, 0)
    for c in range(2):
        o_sum.give_far(c)
        o_sum.give_near(c)
    units = hidden.shape[2]
    for c in range(4):
        cols = slice(c * units // 4, (c + 1) * units // 4)
        dg[cols, :] = mm_tn(hidden[:, :, cols].reshape(length, units // 4), dy[...].reshape(length, width)).astype(BF)
    dn_grad.scatter()

    sm[...] = jnp.zeros(sm.shape, F32)
    for c in range(2):
        cut = halves[c]
        grad = dy[pl.ds(rank, 1), cut][0].astype(F32)
        total = s_sum.total(c)
        normed, scale = norm(middle[cut, :])
        dmiddle[cut, :] = grad + norm_back(total, normed, scale, g2[...])
        low = dmiddle[cut, :].astype(BF)
        dmid[pl.ds(rank, 1), cut] = low[None]
        dmid_all.send(c)
        sm[0:1, :] += jnp.sum(total * normed, 0, keepdims=True)
        sm[1:2, :] += jnp.sum(total, 0, keepdims=True)
        sm[2:3, :] += jnp.sum(low.astype(F32), 0, keepdims=True)
        sm[3:4, :] += jnp.sum(grad, 0, keepdims=True)
    dn_grad.middle()
    for c in range(4):
        cols = slice(c * width // 4, (c + 1) * width // 4)
        ug[cols, :] = mm_tn(second[:, :, cols].reshape(length, width // 4), dpre[...].reshape(length, units)).astype(BF)
    up_grad.scatter()
    bias_sum = jnp.sum(dpre[...].reshape(length, units).astype(F32), 0, keepdims=True)
    for q in range(4):
        sm[8 + q : 9 + q, :] = jnp.where(rank == q, bias_sum, 0.0)
    for t in range(3):
        acc[t] = jnp.zeros((length, share), F32)
    a_sum.finish()

    ctx_cols = slice(3 * share, 4 * share)

    def to_context(k):
        s = pl.ds(p.rank_of(k), 1)
        value = mm_nt(dmid[s][0], ow[...]).astype(BF)
        hidden[s, :, ctx_cols] = value[None]
        for h in range(heads):
            cols = slice(h * HD, (h + 1) * HD)
            product = value[:, cols].astype(F32) * own[s, :, cols][0].astype(F32)
            delta[h, strip(p.rank_of(k)), 0:1] = jnp.sum(product, -1, keepdims=True)

    to_context(0)
    dmid_all.both(dmid_all.near)
    to_context(1)
    dmid_all.both(dmid_all.take)
    o_sum.ship(0)
    o_sum.ship(1)
    to_context(2)
    dmid_all.both(dmid_all.last)
    to_context(3)

    mirror = 1 - p.z // 2
    dn_grad.combine()
    for g in range(4):

        def block(e, carry):
            i = (g + e) + mirror * (3 - g - (g + e))
            j = g + mirror * (3 - (g + e) - g)
            qs, ks = strip(i), strip(j)
            for h in range(heads):
                cols = slice(h * HD, (h + 1) * HD)
                q = mixed[qs, cols]
                k = mixed[ks, share + h * HD : share + (h + 1) * HD]
                v = mixed[ks, 2 * share + h * HD : 2 * share + (h + 1) * HD]
                head = hidden[pl.ds(i, 1), :, 3 * share + h * HD : 3 * share + (h + 1) * HD][0]
                low = probs[h, pl.ds(i * (i + 1) // 2 + j, 1)][0]
                acc[2, ks, cols] += mm_tn(low, head)
                back = (low.astype(F32) * (mm_nt(head, v) - delta[h, qs, 0:1])).astype(BF)
                acc[0, qs, cols] += mm(back, k)
                acc[1, ks, cols] += mm_tn(back, q)
            return carry

        lax.fori_loop(0, 4 - g, block, 0)
        r = g + mirror * (3 - 2 * g)
        total = None
        for t in range(3):
            value = acc[t, strip(r), :]
            low = (value * factor if t < 2 else value).astype(BF)
            hidden[pl.ds(r, 1), :, t * share : (t + 1) * share] = low[None]
            term = mm_nt(low, wq[t])
            total = term if total is None else total + term
        a_part[pl.ds(r, 1)] = total.astype(BF)[None]
        f_sum.done(r)
        if g == 0:
            up_grad.middle()
        if g == 2:
            up_grad.combine()
            for c in range(2):
                cut = halves[c]
                rows_out[1, cut] = (middle[cut, :] + (o_sum.total(c) + dwb[...])).astype(BF)
                put_back(1, output, c)
        if g == 1:
            og[...] = mm_tn(own[...].reshape(length, share), dmid[...].reshape(length, width)).astype(BF)
            ow_grad.scatter()
    p.at_home(dn_grad.final)
    for t in range(3):
        cols = slice(t * share, (t + 1) * share)
        low = hidden[:, :, cols].reshape(length, share)
        pg[t] = mm_tn(first[...].reshape(length, width), low).astype(BF)
        pj_grads[t].scatter()
        bias = jnp.sum(low.astype(F32), 0, keepdims=True)
        line = (6, 7, 12)[t]
        for q in range(4):
            sm[line : line + 1, q * share : (q + 1) * share] = jnp.where(rank == q, bias, 0.0)
    for c in range(2):
        cut = halves[c]
        total = f_sum.total(c)
        normed, scale = norm(xs[cut, :].astype(F32))
        rows_out[0, cut] = (dmiddle[cut, :] + norm_back(total, normed, scale, g1[...])).astype(BF)
        put_back(0, tokens_grad, c)
        sm[4:5, :] += jnp.sum(total * normed, 0, keepdims=True)
        sm[5:6, :] += jnp.sum(total, 0, keepdims=True)

    def sm_copy(k, t):
        return remote(sm, sm_in.at[k], ss_sm.at[k], rs_sm.at[k], p.along(t))

    for k, t in enumerate(others):
        sm_copy(k, t).start()
    late = (ow_grad, *pj_grads)
    p.at_home(dn_grad.relay)
    for grad_sum in late:
        grad_sum.middle()
    p.at_home(up_grad.final)
    for grad_sum in late:
        grad_sum.combine()
    sm_sum = sm[...]
    for k, t in enumerate(others):
        sm_copy(k, t).wait_recv()
        sm_sum = sm_sum + sm_in[k]
    smp[pl.ds(p.d, 1)] = sm_sum[None]
    sm_all = Plane(p, smp, ss_sp, rs_sp)
    sm_all.send()
    p.at_home(dn_grad.relay_last)
    p.at_home(up_grad.relay)
    for grad_sum in late:
        p.at_home(grad_sum.final)
    sm_all.take()
    p.at_home(up_grad.relay_last)
    sm_all.rest()
    small_out[...] = jnp.sum(smp[...], 0)
    for grad_sum in late:
        p.at_home(grad_sum.relay)
    for grad_sum in late:
        p.at_home(grad_sum.relay_last)

    for group in (first_all, second_all, dy_all, dmid_all, s_sum, o_sum, f_sum, sm_all):
        group.finish()
    for k, t in enumerate(others):
        sm_copy(k, t).wait_send()

    @p.at_home
    def _():
        seg_give().wait_send()
        for c in range(2):
            back_home(0, tokens_grad, c).wait()
            back_home(1, output, c).wait()

    @p.if_swapped
    def _():
        for copy in (x_swap(0), x_swap(1), bq_swap(), ub_swap(), cot_swap(rank)):
            copy.wait_send()
        for c in range(2):
            back_swap(0, tokens_grad, c).wait()
            back_swap(1, output, c).wait()
        for move in moves:
            move.finish()

    for grad_sum in (dn_grad, up_grad, ow_grad, *pj_grads):
        grad_sum.finish()


def run_layer(x, cot, seg_ids, g1, b1, wq, bq, ow, ob, g2, b2, upw, upb, dnw, dnb):
    rows, width = x.shape
    share = wq.shape[2]
    length = 4 * rows
    heads = share // HD
    units = upw.shape[1]
    vm = pl.BlockSpec(memory_space=VMEM)
    hbm = pl.BlockSpec(memory_space=pl.ANY)
    token = (rows, width)
    outs = [
        (hbm, token, BF), (hbm, token, BF), (vm, (16, width), F32), (hbm, (3, width, share), BF),
        (hbm, (share, width), BF), (hbm, (width, units), BF), (hbm, (units, width), BF),
    ]
    four = VMEM((4,) + token, BF)
    sums = [VMEM((2,) + token, BF), VMEM(token, BF), VMEM(token, BF)]
    dn_q, up_q, ow_q = (units // 4, width), (width // 4, units), (share // 4, width)
    pj_q = (width // 4, share)
    eighths = [((), (units // 8, width)), ((), (width // 8, units)), ((3,), (width // 8, share)), ((), (share // 8, width))]
    pair = lambda *n: [DMA(n), DMA(n)]
    return pl.pallas_call(
        layer,
        out_shape=[jax.ShapeDtypeStruct(s, t) for _, s, t in outs],
        in_specs=[hbm] * 15,
        out_specs=[m for m, _, _ in outs],
        scratch_shapes=[
            VMEM(token, BF), VMEM((1, length), jnp.int32), VMEM((length, HD), jnp.int32), four, four, four, four,
            VMEM((length, 3 * share), BF), VMEM((4, rows, share), BF), VMEM((heads, 10, rows, rows), BF),
            VMEM((heads, length, 1), F32),
            VMEM((3, width, share), BF), VMEM((3, share), F32), VMEM((share, width), BF), VMEM((width, units), BF),
            VMEM((1, units), F32), VMEM((units, width), BF),
            four, *sums, four, *sums, four, *sums,
            VMEM((4, rows, units), BF), VMEM((4, rows, units), BF),
            VMEM((units, width), BF), VMEM((width, units), BF), VMEM((3, width, share), BF), VMEM((share, width), BF),
            *[VMEM(lead + (2, 2) + q, BF) for lead, q in eighths], *[VMEM(lead + (2,) + q, BF) for lead, q in eighths],
            *2 * [VMEM(dn_q, BF), VMEM(up_q, BF), VMEM((3,) + pj_q, BF), VMEM(ow_q, BF)],
            *6 * [VMEM((1, width), F32)], VMEM((3, length, share), F32), VMEM(token, F32), VMEM(token, F32), VMEM((2,) + token, BF),
            VMEM((16, width), F32), VMEM((3, 16, width), F32), VMEM((8, 16, width), F32),
            DMA((9,)), *pair(13), *pair(3, 2), *pair(3, 2), *pair(3, 2), *pair(3, 2), *pair(3, 2), *pair(3, 2), *pair(3, 2),
            *pair(3, 2), *pair(3, 4, 1), *pair(4, 1), *pair(4, 2), *pair(4, 2), *pair(11, 2), *pair(11, 2), *pair(3, 11, 2), *pair(11, 2),
            *pair(3), *pair(7),
        ],
        compiler_params=pltpu.CompilerParams(collective_id=0, has_side_effects=True, vmem_limit_bytes=64 << 20),
        name="layer",
    )(
        x, cot, seg_ids.reshape(1, length), g1.reshape(1, width), b1.reshape(1, width), wq, bq, ow,
        ob.reshape(1, width), g2.reshape(1, width), b2.reshape(1, width), upw, upb.reshape(1, units), dnw,
        dnb.reshape(1, width),
    )


def widen(sm, out, tg, pg, og, ug, dg, out_o, tg_o, pg_o, og_o, ug_o, dg_o, pb_o, ub_o, *rest):
    for src, dst in ((out, out_o), (tg, tg_o), (pg, pg_o), (og, og_o), (ug, ug_o), (dg, dg_o)):
        dst[...] = src[...].astype(dst.dtype)

    @pl.when(pl.program_id(0) == 0)
    def _():
        z = lax.axis_index("mp")
        share = pb_o.shape[1]
        for t, line in enumerate((6, 7, 12)):
            pb_o[t : t + 1, :] = sm[line : line + 1, pl.ds(pl.multiple_of(z * share, share), share)]
        ub_o[...] = sm[pl.ds(8 + z, 1), :][0]
        for line, dst in enumerate(rest):
            dst[...] = sm[line, :]


def run_widen(sm, out, tg, pg, og, ug, dg):
    steps = 4

    def cut(v, axis):
        shape = list(v.shape)
        shape[axis] //= steps
        return pl.BlockSpec(tuple(shape), lambda i: tuple(i if a == axis else 0 for a in range(v.ndim)))

    def whole(shape):
        return pl.BlockSpec(shape, lambda i: tuple(0 for _ in shape))

    wide = [(out, 0, BF), (tg, 0, BF), (pg, 1, F32), (og, 0, F32), (ug, 0, F32), (dg, 0, F32)]
    width = sm.shape[1]
    small = [(3, pg.shape[2]), (width,)] + [(width,)] * 6
    return pl.pallas_call(
        widen,
        grid=(steps,),
        out_shape=[jax.ShapeDtypeStruct(v.shape, t) for v, _, t in wide] + [jax.ShapeDtypeStruct(s, F32) for s in small],
        in_specs=[whole(sm.shape)] + [cut(v, a) for v, a, _ in wide],
        out_specs=[cut(v, a) for v, a, _ in wide] + [whole(s) for s in small],
        compiler_params=pltpu.CompilerParams(vmem_limit_bytes=60 << 20),
        name="widen",
    )(sm, out, tg, pg, og, ug, dg)


def shards(
    tokens, seg_ids, cotangent, first_gain, first_shift, project_weight, project_bias, out_weight, out_bias,
    second_gain, second_shift, up_weight, up_bias, down_weight, down_bias,
):
    output, tokens_grad, *sums = run_layer(
        tokens, cotangent, seg_ids, first_gain, first_shift, project_weight, project_bias, out_weight, out_bias,
        second_gain, second_shift, up_weight, up_bias, down_weight, down_bias,
    )
    if lax.axis_size("dp") > 8:
        sums = [v.astype(jnp.float32) * 0.125 for v in sums]
        sums = list(lax.psum(tuple(sums), "dp"))
    output, tokens_grad, pg, og, ug, dg, pb, ub, g2g, b2g, obg, dbg, g1g, b1g = run_widen(
        sums[0], output, tokens_grad, *sums[1:]
    )
    return output, tokens_grad, g1g, b1g, pg, pb, og, obg, g2g, b2g, ug, ub, dg, dbg


def solution(mesh):
    in_specs = (
        P(("dp", "mp"), None),
        P("dp"),
        P(("dp", "mp"), None),
        P(),
        P(),
        P(None, None, "mp"),
        P(None, "mp"),
        P("mp", None),
        P(),
        P(),
        P(),
        P(None, "mp"),
        P("mp"),
        P("mp", None),
        P(),
    )
    out_specs = (
        P(("dp", "mp"), None),
        P(("dp", "mp"), None),
        P(),
        P(),
        P(None, None, "mp"),
        P(None, "mp"),
        P("mp", None),
        P(),
        P(),
        P(),
        P(None, "mp"),
        P("mp"),
        P("mp", None),
        P(),
    )
    return jax.shard_map(shards, mesh=mesh, in_specs=in_specs, out_specs=out_specs, check_vma=False)
```

```python
import math

import jax
import jax.numpy as jnp
from jax import lax
from jax.experimental import pallas as pl
from jax.experimental.pallas import tpu as pltpu
from jax.sharding import PartitionSpec as P

HD = 128
EPS = 1e-05
BF = jnp.bfloat16
F32 = jnp.float32
MESH = pl.DeviceIdType.MESH
VMEM = pltpu.VMEM
DMA = pltpu.SemaphoreType.DMA
GELU_A = 0.7978845608
GELU_B = 0.044715


def mm(left, right):
    return jnp.dot(left, right, preferred_element_type=F32)


def mm_nt(left, right):
    return lax.dot_general(left, right, (((1,), (1,)), ((), ())), preferred_element_type=F32)


def mm_tn(left, right):
    return lax.dot_general(left, right, (((0,), (0,)), ((), ())), preferred_element_type=F32)


def remote(src, dst, ss, rs, device):
    return pltpu.make_async_remote_copy(
        src_ref=src, dst_ref=dst, send_sem=ss, recv_sem=rs, device_id=device, device_id_type=MESH
    )


def local(src, dst, sem):
    return pltpu.make_async_copy(src, dst, sem)


def barrier(devices):
    sem = pltpu.get_barrier_semaphore()
    for device in devices:
        pl.semaphore_signal(sem, 1, device_id=device, device_id_type=MESH)
    return lambda: pl.semaphore_wait(sem, len(devices))


def start(copy):
    copy.start()


def wait(copy):
    copy.wait()


def sent(copy):
    copy.wait_send()


def came(copy):
    copy.wait_recv()


def norm(values):
    mean = jnp.mean(values, -1, keepdims=True)
    centered = values - mean
    var = jnp.mean(centered * centered, -1, keepdims=True)
    scale = lax.rsqrt(var + EPS)
    return centered * scale, scale


def norm_back(grad, normed, scale, gain):
    scaled = grad * gain
    return scale * (
        scaled - jnp.mean(scaled, -1, keepdims=True) - normed * jnp.mean(scaled * normed, -1, keepdims=True)
    )


def gelu_parts(v):
    square = v * v
    t = jnp.tanh(GELU_A * v * (1.0 + GELU_B * square))
    half = 0.5 * (1.0 + t)
    slope = half + 0.5 * v * (1.0 - t * t) * (GELU_A * (1.0 + 3.0 * GELU_B * square))
    return v * half, slope


class Place:
    def __init__(self):
        self.z = lax.axis_index("mp")
        self.dp = lax.axis_index("dp")
        self.d = lax.rem(self.dp, 8)
        self.base = self.dp - self.d
        self.core = lax.rem(self.d, 2)
        self.column = self.d // 2
        bit_x = lax.rem(self.column, 2)
        bit_y = self.column // 2
        self.step_x = 1 - 2 * bit_x
        self.step_y = 2 - 4 * bit_y
        self.sibling = self.dp + 1 - 2 * self.core
        self.swapped = lax.rem(self.core + self.z // 2, 2)
        self.far = lax.rem(self.z + 2, 4)
        self.rank = lax.rem(self.z + 2 * self.swapped, 4)
        self.odd = lax.rem(self.z, 2)

    def column_at(self, i):
        return self.column + (i % 2) * self.step_x + (i // 2) * self.step_y

    def chip(self, i):
        return {"dp": self.base + 2 * self.column_at(i) + self.core, "mp": self.z}

    def along(self, z):
        return {"dp": self.dp, "mp": z}

    def to_sibling(self):
        return {"dp": self.sibling, "mp": self.z}

    def across(self):
        return {"dp": self.dp, "mp": self.z + 1 - 2 * self.odd}

    def partner(self):
        return {"dp": self.sibling, "mp": self.far}

    def rank_of(self, k):
        return lax.rem(self.rank + (k // 2) * (1 - 2 * self.odd) + 2 * (k % 2), 4)

    def at_home(self, body):
        pl.when(self.swapped == 0)(body)

    def if_swapped(self, body):
        pl.when(self.swapped == 1)(body)


class Gather:
    def __init__(self, p, buf, ss, rs):
        self.p, self.buf, self.ss, self.rs = p, buf, ss, rs
        self.half = buf.shape[1] // 2

    def _copy(self, k, i, c, device):
        view = self.buf.at[self.p.rank_of(k), pl.ds(c * self.half, self.half)]
        return remote(view, view, self.ss.at[i, c], self.rs.at[i, c], device)

    def send(self, c):
        self._copy(0, 0, c, self.p.across()).start()
        self._copy(0, 1, c, self.p.to_sibling()).start()

    def take(self, c):
        self._copy(2, 0, c, self.p.across()).wait_recv()
        self._copy(2, 2, c, self.p.to_sibling()).start()

    def near(self, c):
        self._copy(1, 1, c, self.p.to_sibling()).wait_recv()

    def last(self, c):
        self._copy(3, 2, c, self.p.to_sibling()).wait_recv()

    def both(self, step):
        step(0)
        step(1)

    def finish(self):
        for c in range(2):
            self._copy(0, 0, c, self.p.across()).wait_send()
            self._copy(0, 1, c, self.p.to_sibling()).wait_send()
            self._copy(2, 2, c, self.p.to_sibling()).wait_send()


class Sum:
    def __init__(self, p, parts, got, out, into, ss, rs):
        self.p, self.parts, self.got, self.out, self.into, self.ss, self.rs = p, parts, got, out, into, ss, rs
        self.half = parts.shape[1] // 2

    def _cut(self, c):
        return pl.ds(c * self.half, self.half)

    def _give(self, n, c):
        src = self.parts.at[self.p.rank_of(1 + 2 * n), self._cut(c)]
        return remote(src, self.got.at[n, self._cut(c)], self.ss.at[n, c], self.rs.at[n, c], self.p.to_sibling())

    def _ship(self, c):
        cut = self._cut(c)
        return remote(self.out.at[cut], self.into.at[cut], self.ss.at[2, c], self.rs.at[2, c], self.p.across())

    def _part(self, k, c):
        return self.parts[pl.ds(self.p.rank_of(k), 1), self._cut(c)][0].astype(F32)

    def give_far(self, c):
        self._give(1, c).start()

    def give_near(self, c):
        self._give(0, c).start()

    def ship(self, c):
        self._give(1, c).wait_recv()
        self.out[self._cut(c), :] = (self._part(2, c) + self.got[1, self._cut(c)].astype(F32)).astype(BF)
        self._ship(c).start()

    def done(self, r):
        for k, step in ((3, self.give_far), (2, self.ship), (1, self.give_near)):

            @pl.when(r == self.p.rank_of(k))
            def _():
                step(0)
                step(1)

    def total(self, c):
        self._give(0, c).wait_recv()
        total = self._part(0, c) + self.got[0, self._cut(c)].astype(F32)
        self._ship(c).wait_recv()
        return total + self.into[self._cut(c), :].astype(F32)

    def finish(self):
        for c in range(2):
            self._give(0, c).wait_send()
            self._give(1, c).wait_send()
            self._ship(c).wait_send()


class Weight:
    def __init__(self, p, src, buf, ss, rs, pieces):
        self.p, self.src, self.buf, self.ss, self.rs, self.pieces = p, src, buf, ss, rs, pieces
        self.size = buf.shape[0] // (4 * pieces)

    def _cut(self, ref, column, n):
        return ref.at[pl.ds(pl.multiple_of((column * self.pieces + n) * self.size, self.size), self.size)]

    def _own(self):
        return local(self.src, self.buf, self.ss.at[0, 0])

    def _swap(self, n):
        src, dst = self._cut(self.src, self.p.column, n), self._cut(self.buf, self.p.column, n)
        return remote(src, dst, self.ss.at[0, n], self.rs.at[0, n], self.p.partner())

    def _share(self, i, column, n):
        view = self._cut(self.buf, column, n)
        return remote(view, view, self.ss.at[i, n], self.rs.at[i, n], self.p.chip(i))

    def home(self):
        self._own().start()

    def swap(self, n=0):
        self._swap(n).start()

    def take(self, n=0):
        self._swap(n).wait_recv()
        for i in (1, 2, 3):
            self._share(i, self.p.column, n).start()

    def ready(self):
        self.p.at_home(lambda: self._own().wait())

        @self.p.if_swapped
        def _():
            for n in range(self.pieces):
                for i in (1, 2, 3):
                    self._share(i, self.p.column_at(i), n).wait_recv()

    def finish(self):
        for n in range(self.pieces):
            self._swap(n).wait_send()
            for i in (1, 2, 3):
                self._share(i, self.p.column, n).wait_send()


class Grad:
    def __init__(self, p, buf, into, last, total, far, out, ss, rs):
        self.p, self.buf, self.into, self.last, self.sum, self.far, self.out = p, buf, into, last, total, far, out
        self.ss, self.rs = ss, rs
        self.size = buf.shape[0] // 8

    def _at(self, ref, column, n):
        return ref.at[pl.ds(pl.multiple_of((2 * column + n) * self.size, self.size), self.size)]

    def _own(self, n):
        return self.sum.at[pl.ds(n * self.size, self.size)]

    def _step(self, n, m):
        return m if n == 0 or m == 3 else 3 - m

    def _column(self, n, m):
        return self.p.column_at(self._step(n, m)) if m else self.p.column

    def _chip(self, n, m):
        return self.p.chip(self._step(n, m))

    def _copy(self, src, dst, i, n, device):
        return remote(src, dst, self.ss.at[i, n], self.rs.at[i, n], device)

    def _first(self, n, k):
        src = self._at(self.buf, self._column(n, (1, 3)[k]), n)
        return self._copy(src, self.into.at[n, k], k, n, self._chip(n, 1))

    def _second(self, n):
        return self._copy(self.into.at[n, 1], self.last.at[n], 2, n, self._chip(n, 2))

    def _home(self):
        return self._copy(self.sum, self.far, 3, 0, self.p.along(self.p.far))

    def _keep(self):
        return local(self.sum, self.out.at[pl.ds(pl.multiple_of(2 * self.p.column * self.size, 2 * self.size), 2 * self.size)], self.ss.at[3, 1])

    def _spread(self, n, m):
        return self._copy(self._own(n), self._at(self.out, self.p.column, n), 3 + m, n, self._chip(n, m))

    def _arrived(self, n, m):
        return self._copy(self._own(n), self._at(self.out, self._column(n, m), n), 3 + m, n, self._chip(n, m))

    def _pass(self, n):
        view = self._at(self.out, self._column(n, 2), n)
        return self._copy(view, view, 6, n, self._chip(n, 1))

    def _passed(self, n):
        view = self._at(self.out, self._column(n, 3), n)
        return self._copy(view, view, 6, n, self._chip(n, 1))

    def _hand(self, n, m):
        view = self._at(self.out, self._column(n, m), n)
        return self._copy(view if m else self._own(n), view, 7 + m, n, self.p.to_sibling())

    def scatter(self):
        for n in range(2):
            self._first(n, 1).start()
            self._first(n, 0).start()

    def middle(self):
        for n in range(2):
            self._first(n, 1).wait_recv()
            value = self._at(self.buf, self._column(n, 2), n)[...].astype(F32) + self.into[n, 1].astype(F32)
            self.into[n, 1] = value.astype(BF)
            self._second(n).start()

    def combine(self):
        for n in range(2):
            self._first(n, 0).wait_recv()
            self._second(n).wait_recv()
            total = self._at(self.buf, self.p.column, n)[...].astype(F32) + self.into[n, 0].astype(F32)
            self._own(n)[...] = (total + self.last[n].astype(F32)).astype(BF)
        self.p.if_swapped(lambda: self._home().start())

    def final(self):
        self._home().wait_recv()
        self.sum[...] = (self.sum[...].astype(F32) + self.far[...].astype(F32)).astype(BF)
        for n in range(2):
            self._spread(n, 2).start()
            self._spread(n, 1).start()
        for n in range(2):
            self._hand(n, 0).start()
        self._keep().start()

    def relay(self):
        for n in range(2):
            self._arrived(n, 2).wait_recv()
            self._pass(n).start()
            self._hand(n, 2).start()

    def relay_last(self):
        for n in range(2):
            self._arrived(n, 1).wait_recv()
            self._hand(n, 1).start()
            self._passed(n).wait_recv()
            self._hand(n, 3).start()

    def finish(self):
        for n in range(2):
            self._first(n, 0).wait_send()
            self._first(n, 1).wait_send()
            self._second(n).wait_send()

        @self.p.at_home
        def _():
            for n in range(2):
                for m in (1, 2):
                    self._spread(n, m).wait_send()
                self._pass(n).wait_send()
                for m in range(4):
                    self._hand(n, m).wait_send()
            self._keep().wait()

        @self.p.if_swapped
        def _():
            self._home().wait_send()
            for n in range(2):
                for m in range(4):
                    self._hand(n, m).wait_recv()


class Plane:
    def __init__(self, p, buf, ss, rs):
        self.p, self.buf, self.ss, self.rs = p, buf, ss, rs

    def _copy(self, column, core, i, device):
        view = self.buf.at[2 * column + core]
        return remote(view, view, self.ss.at[i], self.rs.at[i], device)

    def send(self):
        p = self.p
        for i in (1, 2, 3):
            self._copy(p.column, p.core, i, p.chip(i)).start()
        self._copy(p.column, p.core, 0, p.to_sibling()).start()

    def take(self):
        p = self.p
        for i in (1, 2, 3):
            self._copy(p.column_at(i), p.core, i, p.chip(i)).wait_recv()
            self._copy(p.column_at(i), p.core, 3 + i, p.to_sibling()).start()

    def rest(self):
        p = self.p
        self._copy(p.column, 1 - p.core, 0, p.to_sibling()).wait_recv()
        for i in (1, 2, 3):
            self._copy(p.column_at(i), 1 - p.core, 3 + i, p.to_sibling()).wait_recv()

    def finish(self):
        p = self.p
        self._copy(p.column, p.core, 0, p.to_sibling()).wait_send()
        for i in (1, 2, 3):
            self._copy(p.column, p.core, i, p.chip(i)).wait_send()
            self._copy(p.column_at(i), p.core, 3 + i, p.to_sibling()).wait_send()


def layer(
    x_ref, cot, seg_ref, g1_ref, b1_ref, wq_ref, bq_ref, ow_ref, ob_ref, g2_ref, b2_ref, up_ref, ub_ref, dn_ref, db_ref,
    output, tokens_grad, small_out, pg_out, og_out, ug_out, dg_out,
    xs, seg, segc, first, second, dy, dmid, mixed, own, probs, delta, wq, bq, ow, up, ub, dn,
    a_part, a_got, a_out, a_in, s_part, s_got, s_out, s_in, o_part, o_got, o_out, o_in,
    hidden, dpre, dg, ug, pg, og, dg_in, ug_in, pg_in, og_in, dg_last, ug_last, pg_last, og_last, dg_sum, ug_sum, pg_sum, og_sum,
    dg_far, ug_far, pg_far, og_far, g1, b1, ob, g2, b2, dwb, acc, middle, dmiddle, rows_out, sm, sm_in, smp,
    ss_vec, ss_in, rs_in, ss_first, rs_first, ss_second, rs_second, ss_dy, rs_dy, ss_dmid, rs_dmid,
    ss_a, rs_a, ss_s, rs_s, ss_o, rs_o, ss_f, rs_f, ss_wq, rs_wq, ss_ow, rs_ow, ss_up, rs_up, ss_dn, rs_dn,
    ss_dg, rs_dg, ss_ug, rs_ug, ss_pg, rs_pg, ss_og, rs_og, ss_sm, rs_sm, ss_sp, rs_sp,
):
    p = Place()
    rows, width = xs.shape
    half = rows // 2
    share = wq.shape[2]
    heads = share // HD
    factor = 1.0 / math.sqrt(HD)
    length = 4 * rows
    others = [lax.rem(p.z + k, 4) for k in (1, 2, 3)]
    enter = barrier([p.to_sibling(), p.partner()] + [p.along(t) for t in others] + [p.chip(i) for i in (1, 2, 3)])
    rank = p.rank
    halves = [slice(0, half), slice(half, rows)]

    def strip(index):
        return pl.ds(pl.multiple_of(index * rows, rows), rows)

    wq_moves = [Weight(p, wq_ref.at[t], wq.at[t], ss_wq.at[t], rs_wq.at[t], 1) for t in range(3)]
    ow_move = Weight(p, ow_ref, ow, ss_ow, rs_ow, 1)
    up_move = Weight(p, up_ref, up, ss_up, rs_up, 2)
    dn_move = Weight(p, dn_ref, dn, ss_dn, rs_dn, 2)
    moves = (*wq_moves, ow_move, up_move, dn_move)
    first_all = Gather(p, first, ss_first, rs_first)
    second_all = Gather(p, second, ss_second, rs_second)
    dy_all = Gather(p, dy, ss_dy, rs_dy)
    dmid_all = Gather(p, dmid, ss_dmid, rs_dmid)
    a_sum = Sum(p, a_part, a_got, a_out, a_in, ss_a, rs_a)
    s_sum = Sum(p, s_part, s_got, s_out, s_in, ss_s, rs_s)
    o_sum = Sum(p, o_part, o_got, o_out, o_in, ss_o, rs_o)
    f_sum = Sum(p, a_part, a_got, a_out, a_in, ss_f, rs_f)
    dn_grad = Grad(p, dg, dg_in, dg_last, dg_sum, dg_far, dg_out, ss_dg, rs_dg)
    up_grad = Grad(p, ug, ug_in, ug_last, ug_sum, ug_far, ug_out, ss_ug, rs_ug)
    ow_grad = Grad(p, og, og_in, og_last, og_sum, og_far, og_out, ss_og, rs_og)
    pj_grads = [
        Grad(
            p, pg.at[t], pg_in.at[t], pg_last.at[t], pg_sum.at[t], pg_far.at[t], pg_out.at[t], ss_pg.at[t], rs_pg.at[t]
        )
        for t in range(3)
    ]

    def x_home():
        return local(x_ref, xs, ss_in.at[0])

    def cot_home():
        return local(cot, dy.at[rank], ss_in.at[1])

    def x_swap(c):
        cut = pl.ds(c * half, half)
        return remote(x_ref.at[cut], xs.at[cut], ss_in.at[7 + c], rs_in.at[7 + c], p.partner())

    def cot_swap(slot):
        return remote(cot, dy.at[slot], ss_in.at[1], rs_in.at[1], p.partner())

    def bq_swap():
        return remote(bq_ref, bq, ss_in.at[2], rs_in.at[2], p.partner())

    def ub_swap():
        return remote(ub_ref, ub, ss_in.at[3], rs_in.at[3], p.partner())

    def seg_give():
        return remote(seg_ref, seg, ss_in.at[4], rs_in.at[4], p.to_sibling())

    def back_swap(n, out, c):
        cut = pl.ds(c * half, half)
        i = 9 + 2 * n + c
        return remote(rows_out.at[n, cut], out.at[cut], ss_in.at[i], rs_in.at[i], p.partner())

    def back_home(n, out, c):
        cut = pl.ds(c * half, half)
        return local(rows_out.at[n, cut], out.at[cut], ss_in.at[9 + 2 * n + c])

    def put_back(n, out, c):
        p.at_home(lambda: back_home(n, out, c).start())
        p.if_swapped(lambda: back_swap(n, out, c).start())

    vectors = [
        local(a, b, ss_vec.at[i])
        for i, (a, b) in enumerate(
            ((g1_ref, g1), (b1_ref, b1), (ob_ref, ob), (g2_ref, g2), (b2_ref, b2), (db_ref, dwb))
        )
    ]
    kept = [local(a, b, ss_vec.at[6 + i]) for i, (a, b) in enumerate(((bq_ref, bq), (ub_ref, ub), (seg_ref, seg)))]

    @p.at_home
    def _():
        x_home().start()

    for copy in vectors:
        copy.start()

    @p.at_home
    def _():
        for copy in kept:
            copy.start()
        for move in moves:
            move.home()
        cot_home().start()

    enter()

    @p.if_swapped
    def _():
        x_swap(0).start()
        x_swap(1).start()

    @p.at_home
    def _():
        seg_give().start()
        x_home().wait()
        for copy in kept:
            copy.wait()

    for copy in vectors:
        copy.wait()
    for c in range(2):

        @p.if_swapped
        def _():
            x_swap(c).wait_recv()
            wq_moves[c].swap()

        normed, _ = norm(xs[halves[c], :].astype(F32))
        first[pl.ds(rank, 1), halves[c]] = (normed * g1[...] + b1[...]).astype(BF)[None]
        first_all.send(c)

    @p.if_swapped
    def _():
        bq_swap().start()
        wq_moves[2].swap()
        wq_moves[0].take()
        ow_move.swap()
        wq_moves[1].take()
        ub_swap().start()
        up_move.swap(0)
        wq_moves[2].take()
        up_move.swap(1)
        seg_give().wait_recv()
        bq_swap().wait_recv()

    segc[...] = jnp.transpose(jnp.broadcast_to(seg[0:1, :], (HD, length)))

    def project(k):
        s = p.rank_of(k)
        block = first[pl.ds(s, 1)][0]
        for t in range(3):
            value = mm(block, wq[t]) + bq[t : t + 1, :]
            mixed[strip(s), t * share : (t + 1) * share] = value.astype(BF)

    @p.at_home
    def _():
        for move in wq_moves:
            move.ready()
        project(0)

    first_all.both(first_all.take)

    @p.at_home
    def _():
        project(2)

    @p.if_swapped
    def _():
        for move in wq_moves:
            move.ready()
        project(0)
        project(2)
        ow_move.take()

    first_all.both(first_all.near)
    project(1)
    first_all.both(first_all.last)
    project(3)

    @p.if_swapped
    def _():
        dn_move.swap(0)
        ub_swap().wait_recv()

    @p.at_home
    def _():
        cot_home().wait()
        dy_all.both(dy_all.send)

    ow_move.ready()
    for r in reversed(range(4)):
        span = (r + 1) * rows
        top = r * rows
        place_q = top + lax.broadcasted_iota(jnp.int32, (rows, span), 0)
        place_k = lax.broadcasted_iota(jnp.int32, (rows, span), 1)
        allowed = (segc[top : top + rows, 0:1] == seg[0:1, 0:span]) & (place_q >= place_k)
        for h in range(heads):
            q = mixed[top : top + rows, h * HD : (h + 1) * HD]
            k = mixed[0:span, share + h * HD : share + (h + 1) * HD]
            v = mixed[0:span, 2 * share + h * HD : 2 * share + (h + 1) * HD]
            scores = jnp.where(allowed, mm_nt(q, k) * factor, -1e30)
            expo = jnp.exp(scores - jnp.max(scores, -1, keepdims=True))
            low = (expo / jnp.sum(expo, -1, keepdims=True)).astype(BF)
            for j in range(r + 1):
                probs[h, r * (r + 1) // 2 + j] = low[:, j * rows : (j + 1) * rows]
            own[r, :, h * HD : (h + 1) * HD] = mm(low, v).astype(BF)
        a_part[r] = mm(own[r], ow[...]).astype(BF)
        a_sum.done(r)

    @p.if_swapped
    def _():
        cot_swap(p.z).start()
        dn_move.swap(1)
        up_move.take(0)
        up_move.take(1)

    for c in range(2):
        cut = halves[c]
        middle[cut, :] = xs[cut, :].astype(F32) + (a_sum.total(c) + ob[...])
        normed, _ = norm(middle[cut, :])
        second[pl.ds(rank, 1), cut] = (normed * g2[...] + b2[...]).astype(BF)[None]
        second_all.send(c)

    @p.if_swapped
    def _():
        dn_move.take(0)
        dn_move.take(1)


    up_move.ready()

    class Rows:
        def __init__(self, k):
            late = k // 2
            self.top = p.rank_of(k - late * (k - 2))
            self.low = p.rank_of(k + late * (3 - k))
            self.at_top = pl.ds(pl.multiple_of(late * (k - 2) * half, half), half)
            self.at_low = pl.ds(pl.multiple_of(half - late * (3 - k) * half, half), half)

        def load(self, ref):
            return jnp.concatenate([ref[pl.ds(self.top, 1), self.at_top][0], ref[pl.ds(self.low, 1), self.at_low][0]], 0)

        def store(self, ref, value):
            ref[pl.ds(self.top, 1), self.at_top] = value[None, :half]
            ref[pl.ds(self.low, 1), self.at_low] = value[None, half:]

    def feed(k, carry):
        @pl.when(k == 1)
        def _():
            second_all.both(second_all.near)

        @pl.when(k == 2)
        def _():
            @p.if_swapped
            def _():
                cot_swap(rank).wait_recv()
                dy_all.both(dy_all.send)

            second_all.take(0)
            second_all.last(0)

        @pl.when(k == 3)
        def _():
            second_all.take(1)
            second_all.last(1)

        at = Rows(k)
        value, slope = gelu_parts(mm(at.load(second), up[...]) + ub[...])
        at.store(hidden, value.astype(BF))
        at.store(dpre, slope.astype(BF))
        return carry

    lax.fori_loop(0, 4, feed, 0)

    dn_move.ready()
    dy_all.both(dy_all.take)
    dy_all.both(dy_all.near)
    dy_all.both(dy_all.last)

    def feed_back(n, carry):
        k = 2 + n - 4 * (n // 2)
        at = Rows(k)
        back = (mm_nt(at.load(dy), dn[...]) * at.load(dpre).astype(F32)).astype(BF)
        at.store(dpre, back)
        at.store(s_part, mm_nt(back, up[...]).astype(BF))

        @pl.when(k == 2)
        def _():
            s_sum.give_far(0)

        @pl.when(k == 3)
        def _():
            s_sum.give_far(1)
            s_sum.ship(0)

        @pl.when(k == 0)
        def _():
            s_sum.ship(1)

        @pl.when(k == 1)
        def _():
            s_sum.give_near(0)
            s_sum.give_near(1)

        at.store(o_part, mm(at.load(hidden), dn[...]).astype(BF))
        return carry

    lax.fori_loop(0, 4, feed_back, 0)
    for c in range(2):
        o_sum.give_far(c)
        o_sum.give_near(c)
    units = hidden.shape[2]
    for c in range(4):
        cols = slice(c * units // 4, (c + 1) * units // 4)
        dg[cols, :] = mm_tn(hidden[:, :, cols].reshape(length, units // 4), dy[...].reshape(length, width)).astype(BF)
    dn_grad.scatter()

    sm[...] = jnp.zeros(sm.shape, F32)
    for c in range(2):
        cut = halves[c]
        grad = dy[pl.ds(rank, 1), cut][0].astype(F32)
        total = s_sum.total(c)
        normed, scale = norm(middle[cut, :])
        dmiddle[cut, :] = grad + norm_back(total, normed, scale, g2[...])
        low = dmiddle[cut, :].astype(BF)
        dmid[pl.ds(rank, 1), cut] = low[None]
        dmid_all.send(c)
        sm[0:1, :] += jnp.sum(total * normed, 0, keepdims=True)
        sm[1:2, :] += jnp.sum(total, 0, keepdims=True)
        sm[2:3, :] += jnp.sum(low.astype(F32), 0, keepdims=True)
        sm[3:4, :] += jnp.sum(grad, 0, keepdims=True)
    dn_grad.middle()
    for c in range(4):
        cols = slice(c * width // 4, (c + 1) * width // 4)
        ug[cols, :] = mm_tn(second[:, :, cols].reshape(length, width // 4), dpre[...].reshape(length, units)).astype(BF)
    up_grad.scatter()
    bias_sum = jnp.sum(dpre[...].reshape(length, units).astype(F32), 0, keepdims=True)
    for q in range(4):
        sm[8 + q : 9 + q, :] = jnp.where(rank == q, bias_sum, 0.0)
    for t in range(3):
        acc[t] = jnp.zeros((length, share), F32)
    a_sum.finish()

    ctx_cols = slice(3 * share, 4 * share)

    def to_context(k):
        s = pl.ds(p.rank_of(k), 1)
        value = mm_nt(dmid[s][0], ow[...]).astype(BF)
        hidden[s, :, ctx_cols] = value[None]
        for h in range(heads):
            cols = slice(h * HD, (h + 1) * HD)
            product = value[:, cols].astype(F32) * own[s, :, cols][0].astype(F32)
            delta[h, strip(p.rank_of(k)), 0:1] = jnp.sum(product, -1, keepdims=True)

    to_context(0)
    dmid_all.both(dmid_all.near)
    to_context(1)
    dn_grad.combine()
    dmid_all.both(dmid_all.take)
    to_context(2)
    dmid_all.both(dmid_all.last)
    to_context(3)

    mirror = 1 - p.z // 2
    for g in range(4):

        def block(e, carry):
            i = (g + e) + mirror * (3 - g - (g + e))
            j = g + mirror * (3 - (g + e) - g)
            qs, ks = strip(i), strip(j)
            for h in range(heads):
                cols = slice(h * HD, (h + 1) * HD)
                q = mixed[qs, cols]
                k = mixed[ks, share + h * HD : share + (h + 1) * HD]
                v = mixed[ks, 2 * share + h * HD : 2 * share + (h + 1) * HD]
                head = hidden[pl.ds(i, 1), :, 3 * share + h * HD : 3 * share + (h + 1) * HD][0]
                low = probs[h, pl.ds(i * (i + 1) // 2 + j, 1)][0]
                acc[2, ks, cols] += mm_tn(low, head)
                back = (low.astype(F32) * (mm_nt(head, v) - delta[h, qs, 0:1])).astype(BF)
                acc[0, qs, cols] += mm(back, k)
                acc[1, ks, cols] += mm_tn(back, q)
            return carry

        lax.fori_loop(0, 4 - g, block, 0)
        r = g + mirror * (3 - 2 * g)
        total = None
        for t in range(3):
            value = acc[t, strip(r), :]
            low = (value * factor if t < 2 else value).astype(BF)
            hidden[pl.ds(r, 1), :, t * share : (t + 1) * share] = low[None]
            term = mm_nt(low, wq[t])
            total = term if total is None else total + term
        a_part[pl.ds(r, 1)] = total.astype(BF)[None]
        f_sum.done(r)
        if g == 0:
            up_grad.middle()
        if g == 2:
            up_grad.combine()
            p.at_home(dn_grad.final)
        if g == 1:
            og[...] = mm_tn(own[...].reshape(length, share), dmid[...].reshape(length, width)).astype(BF)
            ow_grad.scatter()
    o_sum.ship(0)
    o_sum.ship(1)
    for t in range(3):
        cols = slice(t * share, (t + 1) * share)
        low = hidden[:, :, cols].reshape(length, share)
        pg[t] = mm_tn(first[...].reshape(length, width), low).astype(BF)
        pj_grads[t].scatter()
        bias = jnp.sum(low.astype(F32), 0, keepdims=True)
        line = (6, 7, 12)[t]
        for q in range(4):
            sm[line : line + 1, q * share : (q + 1) * share] = jnp.where(rank == q, bias, 0.0)
    for c in range(2):
        cut = halves[c]
        total = f_sum.total(c)
        normed, scale = norm(xs[cut, :].astype(F32))
        rows_out[0, cut] = (dmiddle[cut, :] + norm_back(total, normed, scale, g1[...])).astype(BF)
        put_back(0, tokens_grad, c)
        sm[4:5, :] += jnp.sum(total * normed, 0, keepdims=True)
        sm[5:6, :] += jnp.sum(total, 0, keepdims=True)

    def sm_copy(k, t):
        return remote(sm, sm_in.at[k], ss_sm.at[k], rs_sm.at[k], p.along(t))

    for k, t in enumerate(others):
        sm_copy(k, t).start()
    late = (ow_grad, *pj_grads)
    p.at_home(dn_grad.relay)
    for grad_sum in late:
        grad_sum.middle()
    p.at_home(up_grad.final)
    p.at_home(dn_grad.relay_last)
    for grad_sum in late:
        grad_sum.combine()
    for c in range(2):
        cut = halves[c]
        rows_out[1, cut] = (middle[cut, :] + (o_sum.total(c) + dwb[...])).astype(BF)
        put_back(1, output, c)
    sm_sum = sm[...]
    for k, t in enumerate(others):
        sm_copy(k, t).wait_recv()
        sm_sum = sm_sum + sm_in[k]
    smp[pl.ds(p.d, 1)] = sm_sum[None]
    sm_all = Plane(p, smp, ss_sp, rs_sp)
    sm_all.send()
    p.at_home(up_grad.relay)
    for grad_sum in late:
        p.at_home(grad_sum.final)
    sm_all.take()
    p.at_home(up_grad.relay_last)
    sm_all.rest()
    small_out[...] = jnp.sum(smp[...], 0)
    for grad_sum in late:
        p.at_home(grad_sum.relay)
    for grad_sum in late:
        p.at_home(grad_sum.relay_last)

    for group in (first_all, second_all, dy_all, dmid_all, s_sum, o_sum, f_sum, sm_all):
        group.finish()
    for k, t in enumerate(others):
        sm_copy(k, t).wait_send()

    @p.at_home
    def _():
        seg_give().wait_send()
        for c in range(2):
            back_home(0, tokens_grad, c).wait()
            back_home(1, output, c).wait()

    @p.if_swapped
    def _():
        for copy in (x_swap(0), x_swap(1), bq_swap(), ub_swap(), cot_swap(rank)):
            copy.wait_send()
        for c in range(2):
            back_swap(0, tokens_grad, c).wait()
            back_swap(1, output, c).wait()
        for move in moves:
            move.finish()

    for grad_sum in (dn_grad, up_grad, ow_grad, *pj_grads):
        grad_sum.finish()


def run_layer(x, cot, seg_ids, g1, b1, wq, bq, ow, ob, g2, b2, upw, upb, dnw, dnb):
    rows, width = x.shape
    share = wq.shape[2]
    length = 4 * rows
    heads = share // HD
    units = upw.shape[1]
    vm = pl.BlockSpec(memory_space=VMEM)
    hbm = pl.BlockSpec(memory_space=pl.ANY)
    token = (rows, width)
    outs = [
        (hbm, token, BF), (hbm, token, BF), (vm, (16, width), F32), (hbm, (3, width, share), BF),
        (hbm, (share, width), BF), (hbm, (width, units), BF), (hbm, (units, width), BF),
    ]
    four = VMEM((4,) + token, BF)
    sums = [VMEM((2,) + token, BF), VMEM(token, BF), VMEM(token, BF)]
    dn_q, up_q, ow_q = (units // 4, width), (width // 4, units), (share // 4, width)
    pj_q = (width // 4, share)
    eighths = [((), (units // 8, width)), ((), (width // 8, units)), ((3,), (width // 8, share)), ((), (share // 8, width))]
    pair = lambda *n: [DMA(n), DMA(n)]
    return pl.pallas_call(
        layer,
        out_shape=[jax.ShapeDtypeStruct(s, t) for _, s, t in outs],
        in_specs=[hbm] * 15,
        out_specs=[m for m, _, _ in outs],
        scratch_shapes=[
            VMEM(token, BF), VMEM((1, length), jnp.int32), VMEM((length, HD), jnp.int32), four, four, four, four,
            VMEM((length, 3 * share), BF), VMEM((4, rows, share), BF), VMEM((heads, 10, rows, rows), BF),
            VMEM((heads, length, 1), F32),
            VMEM((3, width, share), BF), VMEM((3, share), F32), VMEM((share, width), BF), VMEM((width, units), BF),
            VMEM((1, units), F32), VMEM((units, width), BF),
            four, *sums, four, *sums, four, *sums,
            VMEM((4, rows, units), BF), VMEM((4, rows, units), BF),
            VMEM((units, width), BF), VMEM((width, units), BF), VMEM((3, width, share), BF), VMEM((share, width), BF),
            *[VMEM(lead + (2, 2) + q, BF) for lead, q in eighths], *[VMEM(lead + (2,) + q, BF) for lead, q in eighths],
            *2 * [VMEM(dn_q, BF), VMEM(up_q, BF), VMEM((3,) + pj_q, BF), VMEM(ow_q, BF)],
            *6 * [VMEM((1, width), F32)], VMEM((3, length, share), F32), VMEM(token, F32), VMEM(token, F32), VMEM((2,) + token, BF),
            VMEM((16, width), F32), VMEM((3, 16, width), F32), VMEM((8, 16, width), F32),
            DMA((9,)), *pair(13), *pair(3, 2), *pair(3, 2), *pair(3, 2), *pair(3, 2), *pair(3, 2), *pair(3, 2), *pair(3, 2),
            *pair(3, 2), *pair(3, 4, 1), *pair(4, 1), *pair(4, 2), *pair(4, 2), *pair(11, 2), *pair(11, 2), *pair(3, 11, 2), *pair(11, 2),
            *pair(3), *pair(7),
        ],
        compiler_params=pltpu.CompilerParams(collective_id=0, has_side_effects=True, vmem_limit_bytes=64 << 20),
        name="layer",
    )(
        x, cot, seg_ids.reshape(1, length), g1.reshape(1, width), b1.reshape(1, width), wq, bq, ow,
        ob.reshape(1, width), g2.reshape(1, width), b2.reshape(1, width), upw, upb.reshape(1, units), dnw,
        dnb.reshape(1, width),
    )


def widen(sm, out, tg, pg, og, ug, dg, out_o, tg_o, pg_o, og_o, ug_o, dg_o, pb_o, ub_o, *rest):
    for src, dst in ((out, out_o), (tg, tg_o), (pg, pg_o), (og, og_o), (ug, ug_o), (dg, dg_o)):
        dst[...] = src[...].astype(dst.dtype)

    @pl.when(pl.program_id(0) == 0)
    def _():
        z = lax.axis_index("mp")
        share = pb_o.shape[1]
        for t, line in enumerate((6, 7, 12)):
            pb_o[t : t + 1, :] = sm[line : line + 1, pl.ds(pl.multiple_of(z * share, share), share)]
        ub_o[...] = sm[pl.ds(8 + z, 1), :][0]
        for line, dst in enumerate(rest):
            dst[...] = sm[line, :]


def run_widen(sm, out, tg, pg, og, ug, dg):
    steps = 2

    def cut(v, axis):
        shape = list(v.shape)
        shape[axis] //= steps
        return pl.BlockSpec(tuple(shape), lambda i: tuple(i if a == axis else 0 for a in range(v.ndim)))

    def whole(shape):
        return pl.BlockSpec(shape, lambda i: tuple(0 for _ in shape))

    wide = [(out, 0, BF), (tg, 0, BF), (pg, 1, F32), (og, 0, F32), (ug, 0, F32), (dg, 0, F32)]
    width = sm.shape[1]
    small = [(3, pg.shape[2]), (width,)] + [(width,)] * 6
    return pl.pallas_call(
        widen,
        grid=(steps,),
        out_shape=[jax.ShapeDtypeStruct(v.shape, t) for v, _, t in wide] + [jax.ShapeDtypeStruct(s, F32) for s in small],
        in_specs=[whole(sm.shape)] + [cut(v, a) for v, a, _ in wide],
        out_specs=[cut(v, a) for v, a, _ in wide] + [whole(s) for s in small],
        compiler_params=pltpu.CompilerParams(vmem_limit_bytes=60 << 20),
        name="widen",
    )(sm, out, tg, pg, og, ug, dg)


def shards(
    tokens, seg_ids, cotangent, first_gain, first_shift, project_weight, project_bias, out_weight, out_bias,
    second_gain, second_shift, up_weight, up_bias, down_weight, down_bias,
):
    output, tokens_grad, *sums = run_layer(
        tokens, cotangent, seg_ids, first_gain, first_shift, project_weight, project_bias, out_weight, out_bias,
        second_gain, second_shift, up_weight, up_bias, down_weight, down_bias,
    )
    if lax.axis_size("dp") > 8:
        sums = [v.astype(jnp.float32) * 0.125 for v in sums]
        sums = list(lax.psum(tuple(sums), "dp"))
    output, tokens_grad, pg, og, ug, dg, pb, ub, g2g, b2g, obg, dbg, g1g, b1g = run_widen(
        sums[0], output, tokens_grad, *sums[1:]
    )
    return output, tokens_grad, g1g, b1g, pg, pb, og, obg, g2g, b2g, ug, ub, dg, dbg


def solution(mesh):
    in_specs = (
        P(("dp", "mp"), None),
        P("dp"),
        P(("dp", "mp"), None),
        P(),
        P(),
        P(None, None, "mp"),
        P(None, "mp"),
        P("mp", None),
        P(),
        P(),
        P(),
        P(None, "mp"),
        P("mp"),
        P("mp", None),
        P(),
    )
    out_specs = (
        P(("dp", "mp"), None),
        P(("dp", "mp"), None),
        P(),
        P(),
        P(None, None, "mp"),
        P(None, "mp"),
        P("mp", None),
        P(),
        P(),
        P(),
        P(None, "mp"),
        P("mp"),
        P("mp", None),
        P(),
    )
    return jax.shard_map(shards, mesh=mesh, in_specs=in_specs, out_specs=out_specs, check_vma=False)
```
